32 devices in a mesh: tm: 8 (over z, x), tmpl: 4 (over y, core).
Axes of the slice: x: 2, y: 2, z: 4, core: 2. Of those that a mesh axis runs over, the one named last changes fastest.
Arguments:
- records: float32 [4, 4608, 512], P('tmpl', 'tm'), may hold values from -6 to 6
- band_filter: float32 [65], replicated, may hold values from -0.75 to 0.75
- templates: bfloat16 [1024, 144, 128], P('tmpl'), may hold values from -6 to 6
- destinations: int32 [4, 4608], P('tmpl', 'tm'), may hold values from 0 to 7, as said below
- offsets: int32 [4, 4608], P('tmpl', 'tm'), may hold values from 0 to 294400, as said below
- live_counts: int32 [4, 8], P('tmpl', 'tm'), may hold values from 72 to 576, as said below
Outputs:
- detection: float32 [1024, 8192], P('tmpl', 'tm')
The draws below stay inside these ranges and needn't reach their ends.
Inputs may be any that keep to these rules, and one draw needn't show every extreme that they name: `destinations`: device s's 576 entries of a quarter name every window exactly 72 times, so at most 72 live records go from one device to one window; in each quarter some window has all its entries live on every device. `offsets`: multiples of 512; within a quarter every pair of destination and offset occurs exactly once over all entries of all devices. The live entries of a device are its first live_counts entries; the others are absent records.
All inputs are finite; a program needn't handle non-finite values.
Results may differ from the reference program's by a relative error of at most 0.0029.
Values may be sent and summed in bfloat16 or wider, within the bound.
No kernel may reach another device: no remote copies, remote signals or barrier semaphores. Data moves between devices by JAX's collectives and lax.ppermute only.
A program may use at most 128 MiB of HBM per device.

```python
import jax
import jax.numpy as jnp
from jax import lax

CH = 144
TEMPLATES = 1024
TLEN = 128
RECLEN = 512
DEC = 8
TAPS = 65
SLOTS = 16
CHQ = 36
RMAX = 576
CAP = 72
RAW_WIN = 8192
WIN = 1024
LAGS = 8192
N_TM = 8
N_TMPL = 4


def routing_tables(key):
    key_ids, key_full, key_order, key_count, key_pick = jax.random.split(jax.random.fold_in(key, 7), 5)
    labels = jax.vmap(lambda sub: jax.random.permutation(sub, RMAX))(jax.random.split(key_ids, N_TMPL * N_TM))
    labels = labels.reshape(N_TMPL, N_TM, CAP, N_TM).transpose(0, 3, 1, 2).reshape(N_TMPL, N_TM, RMAX)
    entry = jnp.arange(RMAX, dtype=jnp.int32)
    window_of = entry // CAP
    full_window = jax.random.randint(key_full, (N_TMPL,), 0, N_TM)
    shuffle = jax.vmap(lambda sub: jax.random.permutation(sub, RMAX))(jax.random.split(key_order, N_TMPL * N_TM))
    shuffle = shuffle.reshape(N_TMPL, N_TM, RMAX).astype(jnp.int32)
    score = jnp.where(window_of[None, None, :] == full_window[:, None, None], shuffle - RMAX, shuffle)
    order = jnp.argsort(score, axis=-1, stable=True)
    windows = jnp.take_along_axis(jnp.broadcast_to(window_of, (N_TMPL, N_TM, RMAX)), order, -1)
    chosen = jnp.take_along_axis(labels.astype(jnp.int32), order, -1)
    counts = jax.random.randint(key_count, (N_TMPL, N_TM), CAP, RMAX + 1)
    full_sender = jax.random.randint(key_pick, (N_TMPL,), 0, N_TM)
    senders = jnp.arange(N_TM, dtype=jnp.int32)[None, :]
    counts = jnp.where(senders == full_sender[:, None], RMAX, counts)
    counts = jnp.where(senders == (full_sender[:, None] + 1) % N_TM, CAP, counts)
    return (windows.reshape(N_TMPL, N_TM * RMAX).astype(jnp.int32), (chosen * RECLEN).reshape(N_TMPL, N_TM * RMAX).astype(jnp.int32), counts.astype(jnp.int32))


def draw_destinations(key, part):
    return routing_tables(key)[0]


def draw_offsets(key, part):
    return routing_tables(key)[1]


def draw_live_counts(key, part):
    return routing_tables(key)[2]


def steps_of(key, dims, shards, smallest, top_value):
    def one(dim, parts):
        heights = jax.random.uniform(jax.random.fold_in(jax.random.fold_in(key, 6), dim), (parts,), jnp.float32, smallest / len(shards), top_value / len(shards))
        return jnp.repeat(jnp.exp(heights), dims[dim] // parts).reshape((-1,) + (1,) * (len(dims) - dim - 1))

    gain = one(*shards[0])
    for cut in shards[1:]:
        gain = gain * one(*cut)
    return gain


def scatter_about(rng, dims, scale, bound, cuts=(), kind=jnp.bfloat16):
    entries = scale * jax.random.normal(rng, dims, jnp.float32)
    if cuts:
        entries = entries * steps_of(rng, dims, cuts, -0.22, 0.18)
    return jnp.clip(entries, -bound, bound).astype(kind)


def setup_inputs(seed: int = 0) -> dict:
    splits = jax.random.split(jax.random.key(seed), 7)
    records = scatter_about(splits[0], (N_TMPL, N_TM * RMAX, RECLEN), 1.0, 6.0, ((0, 4), (1, 8)), jnp.float32)
    band_filter = scatter_about(splits[1], (TAPS,), TAPS ** -0.5, 0.75, (), jnp.float32)
    templates = scatter_about(splits[2], (TEMPLATES, CH, TLEN), 1.0, 6.0, ((0, 4),))
    destinations = draw_destinations(jax.random.fold_in(splits[6], 71), 0)
    offsets = draw_offsets(jax.random.fold_in(splits[6], 71), 0)
    live_counts = draw_live_counts(jax.random.fold_in(splits[6], 71), 0)
    return dict(records=records, band_filter=band_filter, templates=templates, destinations=destinations, offsets=offsets, live_counts=live_counts)


EPSILON = 1e-06

def place_rows(target_rows, stored):
    empty = jnp.zeros((N_TM * RMAX + 1, RECLEN), jnp.float32)
    return empty.at[target_rows].set(stored.astype(jnp.float32))

def reference(records, band_filter, templates, destinations, offsets, live_counts):
    entry = jnp.arange(N_TM * RMAX, dtype=jnp.int32) % RMAX
    sender = jnp.arange(N_TM * RMAX, dtype=jnp.int32) // RMAX
    limit = live_counts[:, sender]
    is_live = entry[None, :] < limit
    target = destinations * RMAX + offsets // RECLEN
    target = jnp.where(is_live, target, N_TM * RMAX).astype(jnp.int32)
    placed = jax.vmap(place_rows)(target, records)[:, :-1]
    stream = placed.reshape(N_TMPL, N_TM, CHQ, SLOTS, RECLEN).transpose(0, 2, 1, 3, 4).reshape(CH, N_TM * RAW_WIN)
    stream = jnp.pad(stream, ((0, 0), (0, TAPS - DEC)))
    filtered = jnp.zeros((CH, LAGS), jnp.float32)
    for tap_index in range(TAPS):
        strided = lax.slice(stream, (0, tap_index), (CH, tap_index + DEC * (LAGS - 1) + 1), (1, DEC))
        filtered = filtered + band_filter[tap_index] * strided
    decim = filtered.astype(jnp.bfloat16)
    padded = jnp.pad(decim, ((0, 0), (0, TLEN - 1)))
    wide = templates.astype(jnp.float32)
    tscale = jnp.sqrt(lax.optimization_barrier(jnp.mean(wide * wide, axis=(1, 2))) + EPSILON)
    width = min(16, TLEN)

    def one_window(window):
        piece = lax.dynamic_slice_in_dim(padded, window * WIN, WIN + TLEN - 1, 1).astype(jnp.float32)
        corr = jnp.zeros((TEMPLATES, WIN), jnp.float32)
        for group in range(TLEN // width):
            hankel = jnp.stack([piece[:, shift_at:shift_at + WIN] for shift_at in range(group * width, (group + 1) * width)], 0)
            corr = corr + jnp.einsum('kcj,jct->kt', wide[:, :, group * width:(group + 1) * width], hankel, precision=lax.Precision.HIGHEST)
        power = lax.optimization_barrier(jnp.sum(piece * piece, 0))
        running = jnp.concatenate([jnp.zeros((1,), jnp.float32), jnp.cumsum(power)])
        energy = (running[TLEN:] - running[:WIN]) / (CH * TLEN)
        return corr / (CH * TLEN * tscale[:, None] * jnp.sqrt(energy + EPSILON)[None, :])
    windows = lax.map(one_window, jnp.arange(N_TM, dtype=jnp.int32))
    return windows.transpose(1, 0, 2).reshape(TEMPLATES, LAGS)
```

```python
import functools

import jax
import jax.numpy as jnp
from jax import lax
from jax.experimental import pallas as pl
from jax.experimental.pallas import tpu as pltpu
from jax.sharding import PartitionSpec as P

CH = 144
DEC = 8
TAPS = 65
EPSILON = 1e-06

LANES = 128
CHUNK = 16
HEAD = (TAPS - 1) // DEC
GROUP = 12
MIB = 2**20
BF = jnp.bfloat16
F32 = jnp.float32


def whole(space=pltpu.VMEM):
    return pl.BlockSpec(memory_space=space)


def lane_of(shape):
    return lax.broadcasted_iota(jnp.int32, shape, len(shape) - 1)


def row_of(channel):
    row = channel
    for first in range(GROUP, CH, GROUP):
        row = row + jnp.where(channel >= first, CHUNK - GROUP, 0)
    return row


def flip(values):
    lane = lane_of(values.shape)
    return jnp.take_along_axis(values, lane + (CHUNK - 1) - 2 * (lane % CHUNK), 1)


def turn(rows):
    chunk = lane_of((1, LANES)) // CHUNK
    rows = list(rows)
    step = 1
    while step < len(rows):
        odd = (chunk // step) % 2 == 1
        shift = CHUNK * step
        for low in range(len(rows)):
            if low & step:
                continue
            first, second = rows[low], rows[low + step]
            rows[low] = jnp.where(odd, pltpu.roll(second, shift, 1), first)
            rows[low + step] = jnp.where(odd, second, pltpu.roll(first, LANES - shift, 1))
        step *= 2
    return rows


def pack_kernel(slots, windows, live_ref, record_ref, band_ref, window_ref, start_ref, out_ref, taps, labels):
    entries, rec_len = record_ref.shape[1:]
    span = rec_len // DEC
    capacity = entries // windows
    stride = 2 * capacity
    width = taps.shape[1]

    taps[...] = jnp.zeros_like(taps)
    taps[0:1, 0:TAPS] = band_ref[...].reshape(1, TAPS)
    base = jnp.broadcast_to(taps[0:1, :], taps.shape)
    firsts = list(range(HEAD, HEAD + span, 8)) + [0, span, 0, span, 0]
    bands = [
        pltpu.roll(base, (DEC * first - DEC * HEAD) % width, 1, stride=DEC, stride_axis=0)[:, :rec_len]
        for first in firsts
    ]
    bands.append(jnp.zeros((LANES - 8 * len(firsts), rec_len), F32))
    filters = jnp.concatenate(bands, 0)
    value = lax.dot_general(
        record_ref[0],
        filters,
        (((1,), (1,)), ((), ())),
        precision=lax.Precision.HIGHEST,
        preferred_element_type=F32,
    )
    high = value.astype(BF).astype(F32)
    rest = value - high
    middle = rest.astype(BF).astype(F32)
    low = rest - middle

    window = window_ref[...]
    label = start_ref[...] // rec_len
    channel = label // slots
    slot = label - channel * slots
    labels[...] = jnp.zeros_like(labels)
    mark = span + 5 * HEAD
    labels[mark : mark + 1, 0:entries] = (slot + 1).astype(F32)
    labels[mark + 1 : mark + 2, 0:entries] = row_of(channel).astype(F32)
    marks = labels[...].T[:entries]
    lane = lane_of(value.shape)
    payload = jnp.where(
        lane < span + HEAD,
        high,
        jnp.where(lane < span + 3 * HEAD, middle, jnp.where(lane < mark, low, marks)),
    ).astype(BF)

    live = lane_of((1, entries)) < live_ref[0, 0]
    each = lax.broadcasted_iota(jnp.int32, (windows, entries), 0)
    member = (window == each) & live
    ahead = (window == each + 1) & live & (slot < 3)
    both = jnp.concatenate([jnp.where(member, 1.0, 0.0), jnp.where(ahead, 1.0, 0.0)], 0)
    before = lax.broadcasted_iota(jnp.int32, (entries, entries), 0) <= lane_of((entries, entries))
    count = jnp.dot(both.astype(BF), jnp.where(before, 1.0, 0.0).astype(BF), preferred_element_type=F32)
    first = (each * stride).astype(F32)
    place = jnp.sum(jnp.where(member, count[:windows] + first, 0.0), 0, keepdims=True) - 1.0
    place_ahead = (
        jnp.sum(jnp.where(ahead, count[windows:] + (first + capacity), 0.0), 0, keepdims=True) - 1.0
    )
    total = out_ref.shape[0]
    part = total // 4
    for index in range(4):
        row = (lax.broadcasted_iota(jnp.int32, (part, entries), 0) + index * part).astype(F32)
        chosen = jnp.where((row == place) | (row == place_ahead), 1.0, 0.0).astype(BF)
        out_ref[index * part : (index + 1) * part, :] = jnp.dot(
            chosen, payload, preferred_element_type=F32
        ).astype(BF)


def pack(records, band_filter, windows_of, starts, live, slots, windows):
    entries, rec_len = records.shape[1:]
    return pl.pallas_call(
        functools.partial(pack_kernel, slots, windows),
        out_shape=jax.ShapeDtypeStruct((2 * entries, LANES), BF),
        in_specs=[whole(pltpu.SMEM), whole(), whole(), whole(), whole()],
        out_specs=whole(),
        scratch_shapes=[
            pltpu.VMEM((8, rec_len + LANES), F32),
            pltpu.VMEM((LANES, pl.cdiv(entries, LANES) * LANES), F32),
        ],
        compiler_params=pltpu.CompilerParams(vmem_limit_bytes=24 * MIB),
    )(live, records, band_filter, windows_of, starts)


def arrange_kernel(slots, stride, arrived_ref, out_ref):
    total = arrived_ref.shape[0]
    rows = out_ref.shape[1]
    blocks = out_ref.shape[0] - 1
    span = LANES // 2
    mark = span + 5 * HEAD
    arrived = arrived_ref[...]
    lane = lane_of((8, LANES))
    weigh = jnp.where(lane == mark, float(rows), jnp.where(lane == mark + 1, 1.0, 0.0)).astype(BF)
    name = lax.dot_general(weigh, arrived, (((1,), (1,)), ((), ())), preferred_element_type=F32)[0:1]
    ahead = lane_of((1, total)) % stride >= stride // 2
    target = jnp.where(name > 0, name - rows + jnp.where(ahead, float(slots * rows), 0.0), -1.0)
    held = slots + 3
    row = lax.broadcasted_iota(jnp.int32, (held * rows, total), 0).astype(F32)
    chosen = jnp.where(row == target, 1.0, 0.0).astype(BF)
    placed = jnp.dot(chosen, arrived, preferred_element_type=F32)
    lane = lane_of((rows, LANES))
    own = []
    previous = None
    for slot in range(held):
        part = placed[slot * rows : (slot + 1) * rows]
        summed = (
            part
            + pltpu.roll(part, LANES - 2 * HEAD, 1)
            + pltpu.roll(part, LANES - 4 * HEAD, 1)
        )
        if previous is not None:
            kept, tail = previous
            tail = tail + pltpu.roll(summed, LANES - HEAD, 1)
            own.append(jnp.where(lane < span - HEAD, kept, tail))
        previous = part, summed
    pairs = []
    for index in range(0, slots + 2, 2):
        pairs.append(jnp.where(lane < span, own[index], pltpu.roll(own[index + 1], span, 1)))
    turned = turn(pairs[:blocks])
    for index, value in enumerate(turned + pairs[blocks:]):
        out_ref[index] = flip(value).astype(BF)


def arrange(arrived, slots, stride, rows):
    total = arrived.shape[0]
    return pl.pallas_call(
        functools.partial(arrange_kernel, slots, stride),
        out_shape=jax.ShapeDtypeStruct((slots // 2 + 1, rows, LANES), BF),
        in_specs=[whole()],
        out_specs=whole(),
        compiler_params=pltpu.CompilerParams(vmem_limit_bytes=32 * MIB),
    )(arrived)


def regroup_kernel(template_ref, out_ref, square_ref, wide):
    kept, channels, tlen = template_ref.shape
    wide[...] = template_ref[...].astype(F32).reshape(kept * channels, tlen)
    total = jnp.zeros((kept, tlen), F32)
    for channel in range(channels):
        taps = wide[pl.ds(channel, kept, stride=channels), :]
        total = total + taps * taps
        side = (channel % 2) * tlen
        out_ref[channel // 2, :, side : side + tlen] = taps.astype(BF)
    step = pl.program_id(0)

    @pl.when(step == 0)
    def _():
        square_ref[...] = total

    @pl.when(step > 0)
    def _():
        square_ref[...] += total


def regroup(templates):
    kept, channels, tlen = templates.shape
    return pl.pallas_call(
        regroup_kernel,
        grid=(channels // CHUNK,),
        in_specs=[pl.BlockSpec((kept, CHUNK, tlen), lambda i: (0, i, 0))],
        out_specs=[
            pl.BlockSpec((CHUNK // 2, kept, 2 * tlen), lambda i: (i, 0, 0)),
            pl.BlockSpec((kept, tlen), lambda i: (0, 0)),
        ],
        out_shape=[
            jax.ShapeDtypeStruct((channels // 2, kept, 2 * tlen), BF),
            jax.ShapeDtypeStruct((kept, tlen), F32),
        ],
        scratch_shapes=[pltpu.VMEM((kept * CHUNK, tlen), F32)],
        compiler_params=pltpu.CompilerParams(vmem_limit_bytes=24 * MIB),
    )(templates)


def shifted(here, there, row, out):
    step = lax.broadcasted_iota(jnp.int32, (8, LANES), 0)
    within = lane_of((8, LANES)) % CHUNK
    blocks = out.shape[1] // CHUNK
    for side in range(2):
        for block in range(blocks):
            one = jnp.broadcast_to(here[block, pl.ds(row + side, 1), :], (8, LANES))
            other = jnp.broadcast_to(there[block + 1, pl.ds(row + side, 1), :], (8, LANES))
            halves = [
                pltpu.roll(jnp.where(within < CHUNK - first - step, one, other), first, 1, stride=1, stride_axis=0)
                for first in (0, 8)
            ]
            out[side, CHUNK * block : CHUNK * (block + 1), :] = jnp.concatenate(halves, 0).astype(BF)


def correlate_kernel(
    sample_ref, square_ref, template_ref, out_ref, held, here, there, even, odd, scale, arrivals
):
    quarters, blocks, rows = sample_ref.shape[:3]
    blocks -= 1
    groups = arrivals.shape[0]
    pairs = GROUP // 2
    tlen = square_ref.shape[1]

    def fetch(group):
        part = pl.ds(group * pairs, pairs)
        return pltpu.make_async_copy(template_ref.at[part], held.at[part], arrivals.at[group])

    for group in range(groups):
        fetch(group).start()
    lane = lane_of((1, LANES))
    after_power = jnp.zeros((1, LANES), F32)
    for quarter in range(quarters):
        part = slice(rows * quarter, rows * (quarter + 1))
        after = sample_ref[quarter, blocks].astype(F32)
        after_power = after_power + jnp.sum(after * after, 0, keepdims=True)
        for block in range(blocks):
            value = sample_ref[quarter, block].astype(F32)
            following = jnp.where(
                lane >= LANES - CHUNK,
                pltpu.roll(after, (LANES - CHUNK - CHUNK * block) % LANES, 1),
                pltpu.roll(value, LANES - CHUNK, 1),
            )
            here[block, part] = value
            here[block + blocks, part] = following
            there[block, part] = pltpu.roll(value, LANES - CHUNK, 1)
            there[block + blocks, part] = pltpu.roll(following, LANES - CHUNK, 1)
    power = [jnp.sum(here[block] * here[block], 0, keepdims=True) for block in range(blocks)]
    power = [flip(jnp.broadcast_to(line, (8, LANES)))[0:1] for line in turn(power) + [after_power]]
    later = jnp.concatenate(power[:blocks], 0)
    earlier = jnp.concatenate(power[1:], 0)
    step = 1
    while step < LANES:
        later = later + jnp.where(lane < LANES - step, pltpu.roll(later, LANES - step, 1), 0.0)
        earlier = earlier + jnp.where(lane >= step, pltpu.roll(earlier, step, 1), 0.0)
        step *= 2
    earlier = jnp.where(lane >= 1, pltpu.roll(earlier, 1, 1), 0.0)
    norm = float(CH * tlen)
    scale[...] = lax.rsqrt((later + earlier) / norm + EPSILON) / norm

    def products(*sums):
        shifted(here, there, 0, even)

        def one_group(group, carry):
            fetch(group).wait()
            for pair in range(pairs):
                now, then = (even, odd) if pair % 2 == 0 else (odd, even)
                taps = held[group * pairs + pair]
                for stage in range(2):
                    for unit in range(2):
                        first = 2 * (2 * unit + stage)
                        columns = [
                            jnp.concatenate(
                                [now[side, CHUNK * block : CHUNK * block + tlen, :] for side in range(2)], 0
                            )
                            for block in (first, first + 1)
                        ]
                        pltpu.matmul_push_rhs(jnp.concatenate(columns, 1), stage, unit)
                    for unit in range(2):
                        pltpu.matmul_acc_lhs(sums[2 * unit + stage], taps, load_staged_rhs=stage)
                if pair < pairs - 1:
                    row = group * CHUNK + 2 * (pair + 1)
                else:
                    row = jnp.minimum(group + 1, groups - 1) * CHUNK
                shifted(here, there, row, then)
            return carry

        lax.fori_loop(0, groups, one_group, 0)
        results = []
        for total in sums:
            value = pltpu.matmul_pop(total)
            results += [value[:, :LANES], value[:, LANES:]]
        template_scale = lax.rsqrt(jnp.sum(square_ref[...], 1, keepdims=True) / norm + EPSILON)
        for block, value in enumerate(turn(results)):
            out_ref[:, LANES * block : LANES * (block + 1)] = (
                flip(value) * template_scale * scale[block : block + 1, :]
            )

    kept = out_ref.shape[0]
    pl.run_scoped(
        products, *[pltpu.ACC(unit)((kept, 2 * LANES), F32) for unit in (0, 0, 1, 1)]
    )


def correlate(samples, squares, templates):
    pairs, kept, width = templates.shape
    quarters, blocks, rows = samples.shape[:3]
    blocks -= 1
    tlen = width // 2
    here = pltpu.VMEM((2 * blocks, quarters * rows, LANES), F32)
    shifts = pltpu.VMEM((2, CHUNK * (2 * blocks - 1), LANES), BF)
    return pl.pallas_call(
        correlate_kernel,
        out_shape=jax.ShapeDtypeStruct((kept, blocks * LANES), F32),
        in_specs=[whole(), whole(), whole(pl.ANY)],
        out_specs=whole(),
        scratch_shapes=[
            pltpu.VMEM(templates.shape, BF),
            here,
            here,
            shifts,
            shifts,
            pltpu.VMEM((blocks, LANES), F32),
            pltpu.SemaphoreType.DMA((2 * pairs // GROUP,)),
        ],
        compiler_params=pltpu.CompilerParams(vmem_limit_bytes=48 * MIB),
    )(samples, squares, templates)


def shards(records, band_filter, templates, destinations, offsets, live_counts):
    windows = lax.axis_size("tm")
    quarters = lax.axis_size("tmpl")
    entries, rec_len = records.shape[1:]
    channels = CH // quarters
    slots = entries // channels
    stride = 2 * (entries // windows)
    rows = channels // GROUP * CHUNK
    outgoing = pack(records, band_filter, destinations, offsets, live_counts, slots, windows)
    outgoing = outgoing.reshape(windows, stride, LANES)
    arrived = lax.all_to_all(outgoing, "tm", split_axis=0, concat_axis=0, tiled=True)
    grouped, squares = regroup(templates)
    samples = arrange(arrived.reshape(2 * entries, LANES), slots, stride, rows)
    samples = lax.all_gather(samples, "tmpl", axis=0, tiled=False)
    return correlate(samples, squares, grouped)


def solution(mesh):
    in_specs = (
        P("tmpl", "tm", None),
        P(),
        P("tmpl", None, None),
        P("tmpl", "tm"),
        P("tmpl", "tm"),
        P("tmpl", "tm"),
    )
    out_specs = P("tmpl", "tm")
    inner = jax.shard_map(shards, mesh=mesh, in_specs=in_specs, out_specs=out_specs, check_vma=False)
    return inner
```

```python
import functools

import jax
import jax.numpy as jnp
from jax import lax
from jax.experimental import pallas as pl
from jax.experimental.pallas import tpu as pltpu
from jax.sharding import PartitionSpec as P

CH = 144
DEC = 8
TAPS = 65
EPSILON = 1e-06

LANES = 128
CHUNK = 16
HEAD = (TAPS - 1) // DEC
GROUP = 12
MIB = 2**20
BF = jnp.bfloat16
F32 = jnp.float32


def whole(space=pltpu.VMEM):
    return pl.BlockSpec(memory_space=space)


def lane_of(shape):
    return lax.broadcasted_iota(jnp.int32, shape, len(shape) - 1)


def row_of(channel):
    row = channel
    for first in range(GROUP, CH, GROUP):
        row = row + jnp.where(channel >= first, CHUNK - GROUP, 0)
    return row


def flip(values):
    lane = lane_of(values.shape)
    return jnp.take_along_axis(values, lane + (CHUNK - 1) - 2 * (lane % CHUNK), 1)


def turn(rows):
    chunk = lane_of((1, LANES)) // CHUNK
    rows = list(rows)
    step = 1
    while step < len(rows):
        odd = (chunk // step) % 2 == 1
        shift = CHUNK * step
        for low in range(len(rows)):
            if low & step:
                continue
            first, second = rows[low], rows[low + step]
            rows[low] = jnp.where(odd, pltpu.roll(second, shift, 1), first)
            rows[low + step] = jnp.where(odd, second, pltpu.roll(first, LANES - shift, 1))
        step *= 2
    return rows


def pack_kernel(
    slots,
    windows,
    live_hbm,
    record_hbm,
    band_hbm,
    window_hbm,
    start_hbm,
    out_ref,
    live_ref,
    record_ref,
    band_ref,
    window_ref,
    start_ref,
    taps,
    labels,
    arrivals,
):
    entries, rec_len = record_ref.shape[1:]
    span = rec_len // DEC
    capacity = entries // windows
    stride = 2 * capacity
    width = taps.shape[1]
    copies = [
        pltpu.make_async_copy(source, target, arrivals.at[index])
        for index, (source, target) in enumerate(
            [
                (band_hbm, band_ref),
                (window_hbm, window_ref),
                (start_hbm, start_ref),
                (live_hbm, live_ref),
                (record_hbm, record_ref),
            ]
        )
    ]
    for copy in copies:
        copy.start()

    for copy in copies[:4]:
        copy.wait()
    taps[...] = jnp.zeros_like(taps)
    taps[0:1, 0:TAPS] = band_ref[...].reshape(1, TAPS)
    base = jnp.broadcast_to(taps[0:1, :], taps.shape)
    firsts = list(range(HEAD, HEAD + span, 8)) + [0, span, 0, span, 0]
    bands = [
        pltpu.roll(base, (DEC * first - DEC * HEAD) % width, 1, stride=DEC, stride_axis=0)[:, :rec_len]
        for first in firsts
    ]
    bands.append(jnp.zeros((LANES - 8 * len(firsts), rec_len), F32))
    filters = jnp.concatenate(bands, 0)
    window = window_ref[...]
    label = start_ref[...] // rec_len
    channel = label // slots
    slot = label - channel * slots
    labels[...] = jnp.zeros_like(labels)
    mark = span + 5 * HEAD
    labels[mark : mark + 1, 0:entries] = (slot + 1).astype(F32)
    labels[mark + 1 : mark + 2, 0:entries] = row_of(channel).astype(F32)
    marks = labels[...].T[:entries]
    live = lane_of((1, entries)) < live_ref[0, 0]
    each = lax.broadcasted_iota(jnp.int32, (windows, entries), 0)
    member = (window == each) & live
    ahead = (window == each + 1) & live & (slot < 3)
    both = jnp.concatenate([jnp.where(member, 1.0, 0.0), jnp.where(ahead, 1.0, 0.0)], 0)
    before = lax.broadcasted_iota(jnp.int32, (entries, entries), 0) <= lane_of((entries, entries))
    count = jnp.dot(both.astype(BF), jnp.where(before, 1.0, 0.0).astype(BF), preferred_element_type=F32)
    first = (each * stride).astype(F32)
    place = jnp.sum(jnp.where(member, count[:windows] + first, 0.0), 0, keepdims=True) - 1.0
    place_ahead = (
        jnp.sum(jnp.where(ahead, count[windows:] + (first + capacity), 0.0), 0, keepdims=True) - 1.0
    )
    copies[4].wait()
    value = lax.dot_general(
        record_ref[0],
        filters,
        (((1,), (1,)), ((), ())),
        precision=lax.Precision.HIGHEST,
        preferred_element_type=F32,
    )
    high = value.astype(BF).astype(F32)
    rest = value - high
    middle = rest.astype(BF).astype(F32)
    low = rest - middle

    lane = lane_of(value.shape)
    payload = jnp.where(
        lane < span + HEAD,
        high,
        jnp.where(lane < span + 3 * HEAD, middle, jnp.where(lane < mark, low, marks)),
    ).astype(BF)

    total = out_ref.shape[0]
    part = total // 4
    for index in range(4):
        row = (lax.broadcasted_iota(jnp.int32, (part, entries), 0) + index * part).astype(F32)
        chosen = jnp.where((row == place) | (row == place_ahead), 1.0, 0.0).astype(BF)
        out_ref[index * part : (index + 1) * part, :] = jnp.dot(
            chosen, payload, preferred_element_type=F32
        ).astype(BF)


def pack(records, band_filter, windows_of, starts, live, slots, windows):
    entries, rec_len = records.shape[1:]
    return pl.pallas_call(
        functools.partial(pack_kernel, slots, windows),
        out_shape=jax.ShapeDtypeStruct((2 * entries, LANES), BF),
        in_specs=[whole(pltpu.HBM)] * 5,
        out_specs=whole(),
        scratch_shapes=[
            pltpu.SMEM(live.shape, live.dtype),
            pltpu.VMEM(records.shape, F32),
            pltpu.VMEM(band_filter.shape, F32),
            pltpu.VMEM(windows_of.shape, windows_of.dtype),
            pltpu.VMEM(starts.shape, starts.dtype),
            pltpu.VMEM((8, rec_len + LANES), F32),
            pltpu.VMEM((LANES, pl.cdiv(entries, LANES) * LANES), F32),
            pltpu.SemaphoreType.DMA((5,)),
        ],
        compiler_params=pltpu.CompilerParams(vmem_limit_bytes=60 * MIB),
    )(live, records, band_filter, windows_of, starts)


def arrange_kernel(slots, stride, arrived_ref, after_ref, out_ref):
    del after_ref
    total = arrived_ref.shape[0]
    rows = out_ref.shape[1]
    blocks = out_ref.shape[0] - 1
    span = LANES // 2
    mark = span + 5 * HEAD
    arrived = arrived_ref[...]
    lane = lane_of((8, LANES))
    weigh = jnp.where(lane == mark, float(rows), jnp.where(lane == mark + 1, 1.0, 0.0)).astype(BF)
    name = lax.dot_general(weigh, arrived, (((1,), (1,)), ((), ())), preferred_element_type=F32)[0:1]
    ahead = lane_of((1, total)) % stride >= stride // 2
    target = jnp.where(name > 0, name - rows + jnp.where(ahead, float(slots * rows), 0.0), -1.0)
    held = slots + 3
    row = lax.broadcasted_iota(jnp.int32, (held * rows, total), 0).astype(F32)
    chosen = jnp.where(row == target, 1.0, 0.0).astype(BF)
    placed = jnp.dot(chosen, arrived, preferred_element_type=F32)
    lane = lane_of((rows, LANES))
    own = []
    previous = None
    for slot in range(held):
        part = placed[slot * rows : (slot + 1) * rows]
        summed = (
            part
            + pltpu.roll(part, LANES - 2 * HEAD, 1)
            + pltpu.roll(part, LANES - 4 * HEAD, 1)
        )
        if previous is not None:
            kept, tail = previous
            tail = tail + pltpu.roll(summed, LANES - HEAD, 1)
            own.append(jnp.where(lane < span - HEAD, kept, tail))
        previous = part, summed
    pairs = []
    for index in range(0, slots + 2, 2):
        pairs.append(jnp.where(lane < span, own[index], pltpu.roll(own[index + 1], span, 1)))
    turned = turn(pairs[:blocks])
    for index, value in enumerate(turned + pairs[blocks:]):
        out_ref[index] = flip(value).astype(BF)


def arrange(arrived, after, slots, stride, rows):
    total = arrived.shape[0]
    return pl.pallas_call(
        functools.partial(arrange_kernel, slots, stride),
        out_shape=jax.ShapeDtypeStruct((slots // 2 + 1, rows, LANES), BF),
        in_specs=[whole(), whole(pl.ANY)],
        out_specs=whole(),
        compiler_params=pltpu.CompilerParams(vmem_limit_bytes=50 * MIB),
    )(arrived, after)


def regroup_kernel(template_hbm, out_hbm, held, turned, arrivals, departures):
    kept, channels = template_hbm.shape[:2]

    def fetch(index):
        part = pl.ds(CHUNK * index, CHUNK)
        return pltpu.make_async_copy(template_hbm.at[:, part, :], held.at[:, part, :], arrivals.at[index])

    def send(index):
        part = pl.ds(CHUNK * index, CHUNK)
        return pltpu.make_async_copy(turned.at[part], out_hbm.at[part], departures.at[index])

    parts = channels // CHUNK
    for index in range(parts):
        fetch(index).start()

    def one_part(index, carry):
        fetch(index).wait()
        part = pl.ds(CHUNK * index, CHUNK)
        for first in range(0, kept, CHUNK):
            rows = slice(first, first + CHUNK)
            turned[part, rows, :] = jnp.swapaxes(held[rows, part, :], 0, 1)
        send(index).start()
        return carry

    lax.fori_loop(0, parts, one_part, 0)
    for index in range(parts):
        send(index).wait()


def regroup(templates):
    kept, channels, tlen = templates.shape
    turned = (channels, kept, tlen)
    return pl.pallas_call(
        regroup_kernel,
        in_specs=[whole(pltpu.HBM)],
        out_specs=whole(pltpu.HBM),
        out_shape=jax.ShapeDtypeStruct(turned, BF),
        scratch_shapes=[
            pltpu.VMEM(templates.shape, BF),
            pltpu.VMEM(turned, BF),
            pltpu.SemaphoreType.DMA((channels // CHUNK,)),
            pltpu.SemaphoreType.DMA((channels // CHUNK,)),
        ],
        compiler_params=pltpu.CompilerParams(vmem_limit_bytes=56 * MIB),
        cost_estimate=pl.CostEstimate(flops=2 * templates.size, bytes_accessed=4 * templates.size, transcendentals=0),
    )(templates)


def shifted(here, there, row, out):
    step = lax.broadcasted_iota(jnp.int32, (8, LANES), 0)
    within = lane_of((8, LANES)) % CHUNK
    blocks = out.shape[1] // CHUNK
    for side in range(2):
        for block in range(blocks):
            one = jnp.broadcast_to(here[block, pl.ds(row + side, 1), :], (8, LANES))
            other = jnp.broadcast_to(there[block + 1, pl.ds(row + side, 1), :], (8, LANES))
            halves = [
                pltpu.roll(jnp.where(within < CHUNK - first - step, one, other), first, 1, stride=1, stride_axis=0)
                for first in (0, 8)
            ]
            out[side, CHUNK * block : CHUNK * (block + 1), :] = jnp.concatenate(halves, 0).astype(BF)


def correlate_kernel(steps, begun, *refs):
    refs = list(refs)
    sample_refs = [refs.pop(0) for _ in steps]
    template_hbm = refs.pop(0)
    begun_refs = [refs.pop(0) for _ in range(3 if begun else 0)]
    out_refs = [refs.pop(0) for _ in range(1 if begun else 3)]
    samples, held, *unfolded, even, odd, power, square, total, arrivals, template_arrivals, departures = refs
    unfolded = unfolded[:2], unfolded[2:]
    blocks, rows = samples.shape[1:3]
    blocks -= 1
    count, channels, kept, tlen = held.shape
    pairs = channels // 2
    me = lax.axis_index("tmpl")
    norm = float(CH * tlen)
    lane = lane_of((1, LANES))

    fetches = [
        pltpu.make_async_copy(source, samples.at[index], arrivals.at[index])
        for index, source in enumerate(sample_refs)
    ]
    for fetch in fetches:
        fetch.start()

    def fetch_templates(index):
        first = (me ^ steps[index]) * channels
        return pltpu.make_async_copy(
            template_hbm.at[pl.ds(first, channels)], held.at[index], template_arrivals.at[index]
        )

    for index in range(count):
        fetch_templates(index).start()

    def unfold(index, here, there, block):
        value = samples[index, block].astype(F32)
        after = samples[index, blocks].astype(F32)
        following = jnp.where(
            lane >= LANES - CHUNK,
            pltpu.roll(after, (LANES - CHUNK - CHUNK * block) % LANES, 1),
            pltpu.roll(value, LANES - CHUNK, 1),
        )
        here[block] = value
        here[block + blocks] = following
        there[block] = pltpu.roll(value, LANES - CHUNK, 1)
        there[block + blocks] = pltpu.roll(following, LANES - CHUNK, 1)
        power[block] += jnp.sum((value * value).reshape(rows // 8, 8, LANES), 0)
        if block == 0:
            power[blocks] += jnp.sum((after * after).reshape(rows // 8, 8, LANES), 0)

    def lag_scale():
        lines = [jnp.sum(power[block], 0, keepdims=True) for block in range(blocks + 1)]
        lines = turn(lines[:blocks]) + lines[blocks:]
        lines = [flip(jnp.broadcast_to(line, (8, LANES)))[0:1] for line in lines]
        later = jnp.concatenate(lines[:blocks], 0)
        earlier = jnp.concatenate(lines[1:], 0)
        step = 1
        while step < LANES:
            later = later + jnp.where(lane < LANES - step, pltpu.roll(later, LANES - step, 1), 0.0)
            earlier = earlier + jnp.where(lane >= step, pltpu.roll(earlier, step, 1), 0.0)
            step *= 2
        earlier = jnp.where(lane >= 1, pltpu.roll(earlier, 1, 1), 0.0)
        return lax.rsqrt((later + earlier) / norm + EPSILON) / norm

    def row_at(pair):
        return CHUNK * (2 * pair // GROUP) + 2 * pair % GROUP

    def products(*sums):
        if begun:
            power[...] = begun_refs[1][...]
            square[...] = begun_refs[2][...]
        else:
            power[...] = jnp.zeros_like(power)
            square[...] = jnp.zeros_like(square)
        fetches[0].wait()
        for block in range(blocks):
            unfold(0, *unfolded[0], block)
        shifted(*unfolded[0], 0, even)
        for fetch in fetches[1:]:
            fetch.wait()
        for index in range(count):
            side = index % 2
            fetch_templates(index).wait()
            for pair in range(pairs):
                now, then = (even, odd) if pair % 2 == 0 else (odd, even)
                taps = [held[index, 2 * pair + half] for half in range(2)]
                square[...] += sum(jnp.square(tap.astype(F32)) for tap in taps)
                taps = jnp.concatenate(taps, 1)
                for stage in range(2):
                    for unit in range(2):
                        first = 2 * (2 * unit + stage)
                        columns = [
                            jnp.concatenate(
                                [now[half, CHUNK * block : CHUNK * block + tlen, :] for half in range(2)], 0
                            )
                            for block in (first, first + 1)
                        ]
                        pltpu.matmul_push_rhs(jnp.concatenate(columns, 1), stage, unit)
                    for unit in range(2):
                        pltpu.matmul_acc_lhs(sums[2 * unit + stage], taps, load_staged_rhs=stage)
                if pair < blocks and index < count - 1:
                    unfold(index + 1, *unfolded[1 - side], pair)
                if pair < pairs - 1:
                    shifted(*unfolded[side], row_at(pair + 1), then)
                elif index < count - 1:
                    shifted(*unfolded[1 - side], 0, then)
        results = []
        for index, ref in enumerate(sums):
            value = pltpu.matmul_pop(ref)
            if begun:
                value = value + begun_refs[0][:, 2 * LANES * index : 2 * LANES * (index + 1)]
            results += [value[:, :LANES], value[:, LANES:]]
        if not begun:
            for block, value in enumerate(results):
                out_refs[0][:, LANES * block : LANES * (block + 1)] = value
            out_refs[1][...] = power[...]
            out_refs[2][...] = square[...]
            return
        scale = lag_scale()
        template_scale = lax.rsqrt(jnp.sum(square[...], 1, keepdims=True) / norm + EPSILON)
        height = kept // departures.shape[0]
        copies = []
        for part in range(departures.shape[0]):
            span = slice(part * height, (part + 1) * height)
            for block, value in enumerate(turn([result[span] for result in results])):
                total[span, LANES * block : LANES * (block + 1)] = (
                    flip(value) * template_scale[span] * scale[block : block + 1, :]
                )
            copies.append(pltpu.make_async_copy(total.at[span], out_refs[0].at[span], departures.at[part]))
            copies[-1].start()
        for copy in copies:
            copy.wait()

    pl.run_scoped(
        products, *[pltpu.ACC(unit)((kept, 2 * LANES), F32) for unit in (0, 0, 1, 1)]
    )


def correlate(steps, samples, templates, begun=()):
    channels, kept, tlen = templates.shape
    channels //= lax.axis_size("tmpl")
    blocks, rows = samples[0].shape[:2]
    blocks -= 1
    here = pltpu.VMEM((2 * blocks, rows, LANES), F32)
    shifts = pltpu.VMEM((2, CHUNK * (2 * blocks - 1), LANES), BF)
    result = jax.ShapeDtypeStruct((kept, blocks * LANES), F32)
    power = jax.ShapeDtypeStruct((blocks + 1, 8, LANES), F32)
    square = jax.ShapeDtypeStruct((kept, tlen), F32)
    count = len(steps)
    return pl.pallas_call(
        functools.partial(correlate_kernel, steps, bool(begun)),
        out_shape=result if begun else [result, power, square],
        in_specs=[whole(pl.ANY)] * count + [whole(pltpu.HBM)] + [whole()] * len(begun),
        out_specs=whole(pltpu.HBM) if begun else [whole()] * 3,
        scratch_shapes=[
            pltpu.VMEM((count, *samples[0].shape), BF),
            pltpu.VMEM((count, channels, kept, tlen), BF),
            *[here] * 4,
            shifts,
            shifts,
            pltpu.VMEM(power.shape, F32),
            pltpu.VMEM(square.shape, F32),
            pltpu.VMEM(result.shape if begun else (8, LANES), F32),
            pltpu.SemaphoreType.DMA((count,)),
            pltpu.SemaphoreType.DMA((count,)),
            pltpu.SemaphoreType.DMA((4,)),
        ],
        compiler_params=pltpu.CompilerParams(vmem_limit_bytes=50 * MIB),
        cost_estimate=pl.CostEstimate(
            flops=2 * kept * blocks * LANES * count * channels * tlen,
            bytes_accessed=2 * count * channels * kept * tlen,
            transcendentals=0,
        ),
    )(*samples, templates, *begun)


def shards(records, band_filter, templates, destinations, offsets, live_counts):
    windows = lax.axis_size("tm")
    quarters = lax.axis_size("tmpl")
    entries, rec_len = records.shape[1:]
    channels = CH // quarters
    slots = entries // channels
    stride = 2 * (entries // windows)
    rows = channels // GROUP * CHUNK
    outgoing = pack(records, band_filter, destinations, offsets, live_counts, slots, windows)
    outgoing = outgoing.reshape(windows, stride, LANES)
    arrived = lax.all_to_all(outgoing, "tm", split_axis=0, concat_axis=0, tiled=True)
    grouped = regroup(templates)
    own = arrange(arrived.reshape(2 * entries, LANES), grouped, slots, stride, rows)
    steps = tuple(range(1, quarters))
    samples = [
        lax.ppermute(own, "tmpl", [(source, source ^ step) for source in range(quarters)]) for step in steps
    ]
    begun = correlate((0,), [own], grouped)
    return correlate(steps, samples, grouped, begun)


def solution(mesh):
    in_specs = (
        P("tmpl", "tm", None),
        P(),
        P("tmpl", None, None),
        P("tmpl", "tm"),
        P("tmpl", "tm"),
        P("tmpl", "tm"),
    )
    out_specs = P("tmpl", "tm")
    inner = jax.shard_map(shards, mesh=mesh, in_specs=in_specs, out_specs=out_specs, check_vma=False)
    return inner
```

```python
import functools

import jax
import jax.numpy as jnp
from jax import lax
from jax.experimental import pallas as pl
from jax.experimental.pallas import tpu as pltpu
from jax.sharding import PartitionSpec as P

CH = 144
DEC = 8
TAPS = 65
EPSILON = 1e-06

LANES = 128
CHUNK = 16
HEAD = (TAPS - 1) // DEC
MIB = 2**20
BF = jnp.bfloat16
F32 = jnp.float32


def whole(space=pltpu.VMEM):
    return pl.BlockSpec(memory_space=space)


def lane_of(shape):
    return lax.broadcasted_iota(jnp.int32, shape, len(shape) - 1)


def flip(values):
    lane = lane_of(values.shape)
    return jnp.take_along_axis(values, lane + (CHUNK - 1) - 2 * (lane % CHUNK), 1)


def turn(rows):
    chunk = lane_of((1, LANES)) // CHUNK
    rows = list(rows)
    step = 1
    while step < len(rows):
        odd = (chunk // step) % 2 == 1
        shift = CHUNK * step
        for low in range(len(rows)):
            if low & step:
                continue
            first, second = rows[low], rows[low + step]
            rows[low] = jnp.where(odd, pltpu.roll(second, shift, 1), first)
            rows[low + step] = jnp.where(odd, second, pltpu.roll(first, LANES - shift, 1))
        step *= 2
    return rows


def pack_kernel(
    slots,
    windows,
    live_hbm,
    record_hbm,
    band_hbm,
    window_hbm,
    start_hbm,
    out_ref,
    live_ref,
    record_ref,
    band_ref,
    window_ref,
    start_ref,
    taps,
    labels,
    before,
    arrivals,
):
    entries, rec_len = record_ref.shape[1:]
    span = rec_len // DEC
    capacity = entries // windows
    stride = 2 * capacity
    width = taps.shape[1]
    copies = [
        pltpu.make_async_copy(source, target, arrivals.at[index])
        for index, (source, target) in enumerate(
            [
                (band_hbm, band_ref),
                (window_hbm, window_ref),
                (start_hbm, start_ref),
                (live_hbm, live_ref),
                (record_hbm, record_ref),
            ]
        )
    ]
    for copy in copies:
        copy.start()

    before[...] = jnp.where(
        lax.broadcasted_iota(jnp.int32, before.shape, 0) <= lane_of(before.shape), 1.0, 0.0
    ).astype(BF)
    taps[...] = jnp.zeros_like(taps)
    labels[...] = jnp.zeros_like(labels)
    for copy in copies[:4]:
        copy.wait()
    taps[0:1, 0:TAPS] = band_ref[...].reshape(1, TAPS)
    base = jnp.broadcast_to(taps[0:1, :], taps.shape)
    firsts = list(range(HEAD, HEAD + span, 8)) + [0, span, 0, span, 0]
    bands = [
        pltpu.roll(base, (DEC * first - DEC * HEAD) % width, 1, stride=DEC, stride_axis=0)[:, :rec_len]
        for first in firsts
    ]
    bands.append(jnp.zeros((LANES - 8 * len(firsts), rec_len), F32))
    filters = jnp.concatenate(bands, 0)
    filter_high = filters.astype(BF)
    filter_low = (filters - filter_high.astype(F32)).astype(BF)
    filters = jnp.concatenate([filter_high, filter_low], 0)

    window = window_ref[...]
    label = start_ref[...] // rec_len
    channel = label // slots
    slot = label - channel * slots
    mark = span + 5 * HEAD
    labels[mark : mark + 1, 0:entries] = (slot + 1).astype(F32)
    labels[mark + 1 : mark + 2, 0:entries] = channel.astype(F32)
    marks = labels[...].T[:entries]
    live = lane_of((1, entries)) < live_ref[0, 0]
    each = lax.broadcasted_iota(jnp.int32, (windows, entries), 0)
    member = (window == each) & live
    ahead = (window == each + 1) & live & (slot < 3)
    both = jnp.concatenate([jnp.where(member, 1.0, 0.0), jnp.where(ahead, 1.0, 0.0)], 0)
    count = jnp.dot(both.astype(BF), before[...], preferred_element_type=F32)
    first = (each * stride).astype(F32)
    place = jnp.sum(jnp.where(member, count[:windows] + first, 0.0), 0, keepdims=True) - 1.0
    place_ahead = (
        jnp.sum(jnp.where(ahead, count[windows:] + (first + capacity), 0.0), 0, keepdims=True) - 1.0
    )

    copies[4].wait()
    contract = (((1,), (1,)), ((), ()))
    record = record_ref[0]
    record_high = record.astype(BF)
    record_low = (record - record_high.astype(F32)).astype(BF)
    upper = lax.dot_general(record_high, filters, contract, preferred_element_type=F32)
    lower = lax.dot_general(record_low, filters, contract, preferred_element_type=F32)
    value = upper[:, :LANES] + (upper[:, LANES:] + (lower[:, :LANES] + lower[:, LANES:]))
    high = value.astype(BF).astype(F32)
    rest = value - high
    middle = rest.astype(BF).astype(F32)
    low = rest - middle
    lane = lane_of(value.shape)
    payload = jnp.where(
        lane < span + HEAD,
        high,
        jnp.where(lane < span + 3 * HEAD, middle, jnp.where(lane < mark, low, marks)),
    ).astype(BF)

    total = out_ref.shape[0]
    plain = capacity % 8 == 0
    part = stride if plain else total // 4
    row = lax.broadcasted_iota(jnp.int32, (part, entries), 0).astype(F32)
    for index in range(total // part):
        here, there = place - float(index * part), place_ahead - float(index * part)
        if plain:
            chosen = jnp.concatenate(
                [
                    jnp.where(row[:capacity] == here, 1.0, 0.0),
                    jnp.where(row[capacity:] == there, 1.0, 0.0),
                ],
                0,
            )
        else:
            chosen = jnp.where((row == here) | (row == there), 1.0, 0.0)
        out_ref[index * part : (index + 1) * part, :] = jnp.dot(
            chosen.astype(BF), payload, preferred_element_type=F32
        ).astype(BF)


def pack(records, band_filter, windows_of, starts, live, slots, windows):
    entries, rec_len = records.shape[1:]
    return pl.pallas_call(
        functools.partial(pack_kernel, slots, windows),
        out_shape=jax.ShapeDtypeStruct((2 * entries, LANES), BF),
        in_specs=[whole(pltpu.HBM)] * 5,
        out_specs=whole(),
        scratch_shapes=[
            pltpu.SMEM(live.shape, live.dtype),
            pltpu.VMEM(records.shape, F32),
            pltpu.VMEM(band_filter.shape, F32),
            pltpu.VMEM(windows_of.shape, windows_of.dtype),
            pltpu.VMEM(starts.shape, starts.dtype),
            pltpu.VMEM((8, rec_len + LANES), F32),
            pltpu.VMEM((LANES, pl.cdiv(entries, LANES) * LANES), F32),
            pltpu.VMEM((entries, entries), BF),
            pltpu.SemaphoreType.DMA((5,)),
        ],
        compiler_params=pltpu.CompilerParams(vmem_limit_bytes=60 * MIB),
    )(live, records, band_filter, windows_of, starts)


def arrange_kernel(slots, stride, arrived_ref, template_hbm, out_ref, held_ref, arrival):
    fetch = pltpu.make_async_copy(template_hbm.at[: held_ref.shape[0]], held_ref, arrival)
    fetch.start()
    total = arrived_ref.shape[0]
    channels = out_ref.shape[0]
    rows = pl.cdiv(channels, 8) * 8
    blocks = out_ref.shape[1] // LANES - 1
    span = LANES // 2
    mark = span + 5 * HEAD
    arrived = arrived_ref[...].astype(F32)
    capacity = stride // 2
    lane = lane_of((8, LANES))
    weigh = jnp.where(lane == mark, float(rows), jnp.where(lane == mark + 1, 1.0, 0.0)).astype(BF)
    placed = []
    for side, count in enumerate((slots, 3)):
        values = jnp.concatenate(
            [
                arrived[first : first + capacity]
                for first in range(side * capacity, total, stride)
            ],
            0,
        ).astype(BF)
        name = lax.dot_general(weigh, values, (((1,), (1,)), ((), ())), preferred_element_type=F32)[0:1]
        row = lax.broadcasted_iota(jnp.int32, (count * rows, total // 2), 0).astype(F32)
        chosen = jnp.where(row == name - float(rows), 1.0, 0.0).astype(BF)
        placed.append(jnp.dot(chosen, values, preferred_element_type=F32))
    placed = jnp.concatenate(placed, 0)
    held = slots + 3
    lane = lane_of((rows, LANES))
    own = []
    previous = None
    for slot in range(held):
        part = placed[slot * rows : (slot + 1) * rows]
        summed = (
            part
            + pltpu.roll(part, LANES - 2 * HEAD, 1)
            + pltpu.roll(part, LANES - 4 * HEAD, 1)
        )
        if previous is not None:
            kept, tail = previous
            tail = tail + pltpu.roll(summed, LANES - HEAD, 1)
            own.append(jnp.where(lane < span - HEAD, kept, tail))
        previous = part, summed
    pairs = []
    for index in range(0, slots + 2, 2):
        pairs.append(jnp.where(lane < span, own[index], pltpu.roll(own[index + 1], span, 1)))
    turned = turn(pairs[:blocks])
    for index, value in enumerate(turned + pairs[blocks:]):
        out_ref[:, LANES * index : LANES * (index + 1)] = flip(value)[:channels].astype(BF)
    fetch.wait()


def arrange(arrived, templates, slots, stride, channels):
    return pl.pallas_call(
        functools.partial(arrange_kernel, slots, stride),
        out_shape=[
            jax.ShapeDtypeStruct((channels, (slots // 2 + 1) * LANES), BF),
            jax.ShapeDtypeStruct((channels // 3, *templates.shape[1:]), BF),
        ],
        in_specs=[whole(), whole(pltpu.HBM)],
        out_specs=[whole(), whole()],
        scratch_shapes=[pltpu.SemaphoreType.DMA],
        compiler_params=pltpu.CompilerParams(vmem_limit_bytes=50 * MIB),
    )(arrived, templates)


def regroup_kernel(template_hbm, out_hbm, held, turned, arrivals, departures):
    kept, channels = template_hbm.shape[:2]
    quarter = channels // lax.axis_size("tmpl")
    parts = range(0, channels, CHUNK)

    def fetch(first):
        part = slice(first, first + CHUNK)
        return pltpu.make_async_copy(template_hbm.at[:, part, :], held.at[:, part, :], arrivals.at[first // CHUNK])

    fetches = [fetch(first) for first in parts]
    for copy in fetches:
        copy.start()
    sends = []
    for first, copy in zip(parts, fetches):
        copy.wait()
        for row in range(0, kept, CHUNK):
            rows = slice(row, row + CHUNK)
            turned[first : first + CHUNK, rows, :] = jnp.swapaxes(held[rows, first : first + CHUNK, :], 0, 1)
        if first == 0:
            me = lax.axis_index("tmpl")
        edge = min((first // quarter + 1) * quarter, first + CHUNK)
        for start, stop in ((first, edge), (edge, first + CHUNK)):
            if start == stop:
                continue
            place = (me ^ (start // quarter)) * quarter + start % quarter
            sends.append(
                pltpu.make_async_copy(
                    turned.at[start:stop], out_hbm.at[pl.ds(place, stop - start)], departures.at[len(sends)]
                )
            )
            sends[-1].start()
    for copy in sends:
        copy.wait()


def regroup(templates):
    kept, channels, tlen = templates.shape
    turned = (channels, kept, tlen)
    return pl.pallas_call(
        regroup_kernel,
        in_specs=[whole(pltpu.HBM)],
        out_specs=whole(pltpu.HBM),
        out_shape=jax.ShapeDtypeStruct(turned, BF),
        scratch_shapes=[
            pltpu.VMEM(templates.shape, BF),
            pltpu.VMEM(turned, BF),
            pltpu.SemaphoreType.DMA((channels // CHUNK,)),
            pltpu.SemaphoreType.DMA((channels // CHUNK + lax.axis_size("tmpl"),)),
        ],
        compiler_params=pltpu.CompilerParams(vmem_limit_bytes=56 * MIB),
        cost_estimate=pl.CostEstimate(flops=2 * templates.size, bytes_accessed=4 * templates.size, transcendentals=0),
    )(templates)


def shifted(here, there, row, out):
    step = lax.broadcasted_iota(jnp.int32, (8, LANES), 0)
    within = lane_of((8, LANES)) % CHUNK
    blocks = out.shape[1] // CHUNK
    for side in range(2):
        for block in range(blocks):
            one = jnp.broadcast_to(here[block, pl.ds(row + side, 1), :], (8, LANES))
            other = jnp.broadcast_to(there[block + 1, pl.ds(row + side, 1), :], (8, LANES))
            halves = [
                pltpu.roll(jnp.where(within < CHUNK - first - step, one, other), first, 1, stride=1, stride_axis=0)
                for first in (0, 8)
            ]
            out[side, CHUNK * block : CHUNK * (block + 1), :] = jnp.concatenate(halves, 0).astype(BF)


def correlate_kernel(steps, begun, *refs):
    refs = list(refs)
    samples = [refs.pop(0) for _ in steps]
    template_hbm = refs.pop(0)
    first_ref = refs.pop(0)
    begun_refs = [refs.pop(0) for _ in range(3 if begun else 0)]
    out_refs = [refs.pop(0) for _ in range(1 if begun else 4)]
    held, *unfolded, even, odd, power, square, total, arrivals, departures = refs
    unfolded = unfolded[:2], unfolded[2:]
    rows = samples[0].shape[0]
    blocks = samples[0].shape[1] // LANES - 1
    channels, kept, tlen = held.shape[1:]
    pairs = channels // 2
    count = len(steps)
    norm = float(CH * tlen)
    lane = lane_of((1, LANES))

    def fetch(start, stop, target, index):
        return pltpu.make_async_copy(template_hbm.at[start:stop], target, arrivals.at[index])

    early = first_ref.shape[0]
    templates = [first_ref] + [held.at[index] for index in range(count - 1)]
    if begun:
        fetches = [
            fetch(step * channels, (step + 1) * channels, held.at[index], index)
            for index, step in enumerate(steps[1:])
        ]
    else:
        fetches = [
            fetch(early, channels, held.at[0, pl.ds(0, channels - early)], 0),
            fetch(channels, 2 * channels, out_refs[3], 1),
        ]
    for copy in fetches if begun else fetches[:1]:
        copy.start()

    def taps_of(index, channel):
        if not begun and channel >= early:
            return held[0, channel - early]
        return templates[index][channel]

    def unfold(index, here, there, block):
        value = samples[index][:, LANES * block : LANES * (block + 1)].astype(F32)
        after = samples[index][:, LANES * blocks :].astype(F32)
        following = jnp.where(
            lane >= LANES - CHUNK,
            pltpu.roll(after, (LANES - CHUNK - CHUNK * block) % LANES, 1),
            pltpu.roll(value, LANES - CHUNK, 1),
        )
        here[block] = value
        here[block + blocks] = following
        there[block] = pltpu.roll(value, LANES - CHUNK, 1)
        there[block + blocks] = pltpu.roll(following, LANES - CHUNK, 1)
        power[block : block + 1] += jnp.sum(value * value, 0, keepdims=True)
        if block == 0:
            power[blocks:] += jnp.sum(after * after, 0, keepdims=True)

    def lag_scale():
        lines = [power[block : block + 1] for block in range(blocks + 1)]
        lines = turn(lines[:blocks]) + lines[blocks:]
        lines = [flip(jnp.broadcast_to(line, (8, LANES)))[0:1] for line in lines]
        later = jnp.concatenate(lines[:blocks], 0)
        earlier = jnp.concatenate(lines[1:], 0)
        step = 1
        while step < LANES:
            later = later + jnp.where(lane < LANES - step, pltpu.roll(later, LANES - step, 1), 0.0)
            earlier = earlier + jnp.where(lane >= step, pltpu.roll(earlier, step, 1), 0.0)
            step *= 2
        earlier = jnp.where(lane >= 1, pltpu.roll(earlier, 1, 1), 0.0)
        return lax.rsqrt((later + earlier) / norm + EPSILON) / norm

    def products(*sums):
        if begun:
            power[...] = begun_refs[1][...]
            square[...] = begun_refs[2][...]
        else:
            power[...] = jnp.zeros_like(power)
            square[...] = jnp.zeros_like(square)
        for block in range(blocks):
            unfold(0, *unfolded[0], block)
        shifted(*unfolded[0], 0, even)
        for index in range(count):
            side = index % 2
            if index > 0:
                fetches[index - 1].wait()
            for pair in range(pairs):
                now, then = (even, odd) if pair % 2 == 0 else (odd, even)
                if not begun and 2 * pair == early:
                    fetches[0].wait()
                    fetches[1].start()
                taps = [taps_of(index, 2 * pair + half) for half in range(2)]
                square[...] += sum(jnp.square(tap.astype(F32)) for tap in taps)
                taps = jnp.concatenate(taps, 1)
                for stage in range(2):
                    for unit in range(2):
                        first = 2 * (2 * unit + stage)
                        columns = [
                            jnp.concatenate(
                                [now[half, CHUNK * block : CHUNK * block + tlen, :] for half in range(2)], 0
                            )
                            for block in (first, first + 1)
                        ]
                        pltpu.matmul_push_rhs(jnp.concatenate(columns, 1), stage, unit)
                    for unit in range(2):
                        pltpu.matmul_acc_lhs(sums[2 * unit + stage], taps, load_staged_rhs=stage)
                if pair < blocks and index < count - 1:
                    unfold(index + 1, *unfolded[1 - side], pair)
                if pair < pairs - 1:
                    shifted(*unfolded[side], 2 * (pair + 1), then)
                elif index < count - 1:
                    shifted(*unfolded[1 - side], 0, then)
        results = []
        for index, ref in enumerate(sums):
            value = pltpu.matmul_pop(ref)
            if begun:
                value = value + begun_refs[0][:, 2 * LANES * index : 2 * LANES * (index + 1)]
            results += [value[:, :LANES], value[:, LANES:]]
        if not begun:
            for block, value in enumerate(results):
                out_refs[0][:, LANES * block : LANES * (block + 1)] = value
            out_refs[1][...] = power[...]
            out_refs[2][...] = square[...]
            fetches[1].wait()
            return
        scale = lag_scale()
        template_scale = lax.rsqrt(jnp.sum(square[...], 1, keepdims=True) / norm + EPSILON)
        height = kept // departures.shape[0]
        copies = []
        for part in range(departures.shape[0]):
            span = slice(part * height, (part + 1) * height)
            for block, value in enumerate(turn([result[span] for result in results])):
                total[span, LANES * block : LANES * (block + 1)] = (
                    flip(value) * template_scale[span] * scale[block : block + 1, :]
                )
            copies.append(pltpu.make_async_copy(total.at[span], out_refs[0].at[span], departures.at[part]))
            copies[-1].start()
        for copy in copies:
            copy.wait()

    pl.run_scoped(
        products, *[pltpu.ACC(unit)((kept, 2 * LANES), F32) for unit in (0, 0, 1, 1)]
    )


def correlate(steps, samples, templates, first, begun=()):
    channels, kept, tlen = templates.shape
    channels //= lax.axis_size("tmpl")
    rows = samples[0].shape[0]
    blocks = samples[0].shape[1] // LANES - 1
    here = pltpu.VMEM((2 * blocks, rows, LANES), F32)
    shifts = pltpu.VMEM((2, CHUNK * (2 * blocks - 1), LANES), BF)
    result = jax.ShapeDtypeStruct((kept, blocks * LANES), F32)
    power = jax.ShapeDtypeStruct((blocks + 1, LANES), F32)
    square = jax.ShapeDtypeStruct((kept, tlen), F32)
    count = len(steps)
    held = (channels, kept, tlen)
    return pl.pallas_call(
        functools.partial(correlate_kernel, steps, bool(begun)),
        out_shape=result if begun else [result, power, square, jax.ShapeDtypeStruct(held, BF)],
        in_specs=[whole()] * count + [whole(pltpu.HBM)] + [whole()] * (1 + len(begun)),
        out_specs=whole(pltpu.HBM) if begun else [whole()] * 4,
        scratch_shapes=[
            pltpu.VMEM((max(count - 1, 1), *held), BF),
            *[here] * 4,
            shifts,
            shifts,
            pltpu.VMEM(power.shape, F32),
            pltpu.VMEM(square.shape, F32),
            pltpu.VMEM(result.shape if begun else (8, LANES), F32),
            pltpu.SemaphoreType.DMA((2,)),
            pltpu.SemaphoreType.DMA((4,)),
        ],
        compiler_params=pltpu.CompilerParams(vmem_limit_bytes=(50 if begun else 46) * MIB),
        cost_estimate=pl.CostEstimate(
            flops=2 * kept * blocks * LANES * count * channels * tlen,
            bytes_accessed=2 * count * channels * kept * tlen,
            transcendentals=0,
        ),
    )(*samples, templates, first, *begun)


def shards(records, band_filter, templates, destinations, offsets, live_counts):
    windows = lax.axis_size("tm")
    quarters = lax.axis_size("tmpl")
    entries, rec_len = records.shape[1:]
    channels = CH // quarters
    slots = entries // channels
    stride = 2 * (entries // windows)
    outgoing = pack(records, band_filter, destinations, offsets, live_counts, slots, windows)
    outgoing = outgoing.reshape(windows, stride, LANES)
    arrived = lax.all_to_all(outgoing, "tm", split_axis=0, concat_axis=0, tiled=True)
    grouped = regroup(templates)
    own, first = arrange(arrived.reshape(2 * entries, LANES), grouped, slots, stride, channels)
    steps = tuple(range(1, quarters))
    samples = [
        lax.ppermute(own, "tmpl", [(source, source ^ step) for source in range(quarters)]) for step in steps
    ]
    *begun, first = correlate((0,), [own], grouped, first)
    return correlate(steps, samples, grouped, first, begun)


def solution(mesh):
    in_specs = (
        P("tmpl", "tm", None),
        P(),
        P("tmpl", None, None),
        P("tmpl", "tm"),
        P("tmpl", "tm"),
        P("tmpl", "tm"),
    )
    out_specs = P("tmpl", "tm")
    inner = jax.shard_map(shards, mesh=mesh, in_specs=in_specs, out_specs=out_specs, check_vma=False)
    return inner
```

```python
import functools

import jax
import jax.numpy as jnp
from jax import lax
from jax.experimental import pallas as pl
from jax.experimental.pallas import tpu as pltpu
from jax.sharding import PartitionSpec as P

CH = 144
DEC = 8
TAPS = 65
EPSILON = 1e-06

LANES = 128
CHUNK = 16
HEAD = (TAPS - 1) // DEC
MIB = 2**20
BF = jnp.bfloat16
F32 = jnp.float32


def whole(space=pltpu.VMEM):
    return pl.BlockSpec(memory_space=space)


def lane_of(shape):
    return lax.broadcasted_iota(jnp.int32, shape, len(shape) - 1)


def flip(values):
    lane = lane_of(values.shape)
    return jnp.take_along_axis(values, lane + (CHUNK - 1) - 2 * (lane % CHUNK), 1)


def turn(rows):
    chunk = lane_of((1, LANES)) // CHUNK
    rows = list(rows)
    step = 1
    while step < len(rows):
        odd = (chunk // step) % 2 == 1
        shift = CHUNK * step
        for low in range(len(rows)):
            if low & step:
                continue
            first, second = rows[low], rows[low + step]
            rows[low] = jnp.where(odd, pltpu.roll(second, shift, 1), first)
            rows[low + step] = jnp.where(odd, second, pltpu.roll(first, LANES - shift, 1))
        step *= 2
    return rows


def pack_kernel(
    slots,
    windows,
    live_hbm,
    record_hbm,
    band_hbm,
    window_hbm,
    start_hbm,
    out_hbm,
    live_ref,
    record_ref,
    band_ref,
    window_ref,
    start_ref,
    taps,
    labels,
    before,
    out_ref,
    arrivals,
    departures,
):
    entries, rec_len = record_ref.shape[1:]
    span = rec_len // DEC
    capacity = entries // windows
    stride = 2 * capacity
    width = taps.shape[1]
    halves = [pl.ds(first, entries // 2) for first in (0, entries // 2)]
    copies = [
        pltpu.make_async_copy(source, target, arrivals.at[index])
        for index, (source, target) in enumerate(
            [
                (band_hbm, band_ref),
                (window_hbm, window_ref),
                (start_hbm, start_ref),
                (live_hbm, live_ref),
                *[(record_hbm.at[:, rows], record_ref.at[:, rows]) for rows in halves],
            ]
        )
    ]
    for copy in copies:
        copy.start()

    before[...] = jnp.where(
        lax.broadcasted_iota(jnp.int32, before.shape, 0) <= lane_of(before.shape), 1.0, 0.0
    ).astype(BF)
    taps[...] = jnp.zeros_like(taps)
    labels[...] = jnp.zeros_like(labels)
    for copy in copies[:4]:
        copy.wait()
    taps[0:1, 0:TAPS] = band_ref[...].reshape(1, TAPS)
    base = jnp.broadcast_to(taps[0:1, :], taps.shape)
    firsts = list(range(HEAD, HEAD + span, 8)) + [0, span, 0, span, 0]
    bands = [
        pltpu.roll(base, (DEC * first - DEC * HEAD) % width, 1, stride=DEC, stride_axis=0)[:, :rec_len]
        for first in firsts
    ]
    bands.append(jnp.zeros((LANES - 8 * len(firsts), rec_len), F32))
    filters = jnp.concatenate(bands, 0)
    filter_high = filters.astype(BF)
    filter_low = (filters - filter_high.astype(F32)).astype(BF)
    filters = jnp.concatenate([filter_high, filter_low], 0)

    window = window_ref[...]
    label = start_ref[...] // rec_len
    channel = label // slots
    slot = label - channel * slots
    mark = span + 5 * HEAD
    labels[mark : mark + 1, 0:entries] = (slot + 1).astype(F32)
    labels[mark + 1 : mark + 2, 0:entries] = channel.astype(F32)
    marks = labels[...].T[:entries]
    live = lane_of((1, entries)) < live_ref[0, 0]
    each = lax.broadcasted_iota(jnp.int32, (windows, entries), 0)
    member = (window == each) & live
    ahead = (window == each + 1) & live & (slot < 3)
    both = jnp.concatenate([jnp.where(member, 1.0, 0.0), jnp.where(ahead, 1.0, 0.0)], 0)
    count = jnp.dot(both.astype(BF), before[...], preferred_element_type=F32)
    first = (each * stride).astype(F32)
    place = jnp.sum(jnp.where(member, count[:windows] + first, 0.0), 0, keepdims=True) - 1.0
    place_ahead = (
        jnp.sum(jnp.where(ahead, count[windows:] + (first + capacity), 0.0), 0, keepdims=True) - 1.0
    )

    contract = (((1,), (1,)), ((), ()))
    values = []
    for rows, copy in zip(halves, copies[4:]):
        copy.wait()
        record = record_ref[0, rows]
        record_high = record.astype(BF)
        record_low = (record - record_high.astype(F32)).astype(BF)
        upper = lax.dot_general(record_high, filters, contract, preferred_element_type=F32)
        lower = lax.dot_general(record_low, filters, contract, preferred_element_type=F32)
        values.append(upper[:, :LANES] + (upper[:, LANES:] + (lower[:, :LANES] + lower[:, LANES:])))
    value = jnp.concatenate(values, 0)
    high = value.astype(BF).astype(F32)
    rest = value - high
    middle = rest.astype(BF).astype(F32)
    low = rest - middle
    lane = lane_of(value.shape)
    payload = jnp.where(
        lane < span + HEAD,
        high,
        jnp.where(lane < span + 3 * HEAD, middle, jnp.where(lane < mark, low, marks)),
    ).astype(BF)

    total = out_ref.shape[0]
    plain = capacity % 8 == 0
    part = stride if plain else total // 4
    row = lax.broadcasted_iota(jnp.int32, (part, entries), 0).astype(F32)
    sends = []
    for index in range(total // part):
        here, there = place - float(index * part), place_ahead - float(index * part)
        if plain:
            chosen = jnp.concatenate(
                [
                    jnp.where(row[:capacity] == here, 1.0, 0.0),
                    jnp.where(row[capacity:] == there, 1.0, 0.0),
                ],
                0,
            )
        else:
            chosen = jnp.where((row == here) | (row == there), 1.0, 0.0)
        out_ref[index * part : (index + 1) * part, :] = jnp.dot(
            chosen.astype(BF), payload, preferred_element_type=F32
        ).astype(BF)
        span_of = pl.ds(index * part, part)
        sends.append(pltpu.make_async_copy(out_ref.at[span_of], out_hbm.at[span_of], departures.at[index]))
        sends[-1].start()
    for copy in sends:
        copy.wait()


def pack(records, band_filter, windows_of, starts, live, slots, windows):
    entries, rec_len = records.shape[1:]
    return pl.pallas_call(
        functools.partial(pack_kernel, slots, windows),
        out_shape=jax.ShapeDtypeStruct((2 * entries, LANES), BF),
        in_specs=[whole(pltpu.HBM)] * 5,
        out_specs=whole(pltpu.HBM),
        scratch_shapes=[
            pltpu.SMEM(live.shape, live.dtype),
            pltpu.VMEM(records.shape, F32),
            pltpu.VMEM(band_filter.shape, F32),
            pltpu.VMEM(windows_of.shape, windows_of.dtype),
            pltpu.VMEM(starts.shape, starts.dtype),
            pltpu.VMEM((8, rec_len + LANES), F32),
            pltpu.VMEM((LANES, pl.cdiv(entries, LANES) * LANES), F32),
            pltpu.VMEM((entries, entries), BF),
            pltpu.VMEM((2 * entries, LANES), BF),
            pltpu.SemaphoreType.DMA((6,)),
            pltpu.SemaphoreType.DMA((max(windows, 4),)),
        ],
        compiler_params=pltpu.CompilerParams(vmem_limit_bytes=60 * MIB),
    )(live, records, band_filter, windows_of, starts)


def arrange_kernel(slots, stride, arrived_ref, template_hbm, out_ref, held_ref, arrival):
    fetch = pltpu.make_async_copy(template_hbm.at[: held_ref.shape[0]], held_ref, arrival)
    fetch.start()
    total = arrived_ref.shape[0]
    channels = out_ref.shape[0]
    rows = pl.cdiv(channels, 8) * 8
    blocks = out_ref.shape[1] // LANES - 1
    span = LANES // 2
    mark = span + 5 * HEAD
    arrived = arrived_ref[...].astype(F32)
    capacity = stride // 2
    lane = lane_of((8, LANES))
    weigh = jnp.where(lane == mark, float(rows), jnp.where(lane == mark + 1, 1.0, 0.0)).astype(BF)
    placed = []
    for side, count in enumerate((slots, 3)):
        values = jnp.concatenate(
            [
                arrived[first : first + capacity]
                for first in range(side * capacity, total, stride)
            ],
            0,
        ).astype(BF)
        name = lax.dot_general(weigh, values, (((1,), (1,)), ((), ())), preferred_element_type=F32)[0:1]
        row = lax.broadcasted_iota(jnp.int32, (count * rows, total // 2), 0).astype(F32)
        chosen = jnp.where(row == name - float(rows), 1.0, 0.0).astype(BF)
        placed.append(jnp.dot(chosen, values, preferred_element_type=F32))
    placed = jnp.concatenate(placed, 0)
    held = slots + 3
    lane = lane_of((rows, LANES))
    own = []
    previous = None
    for slot in range(held):
        part = placed[slot * rows : (slot + 1) * rows]
        summed = (
            part
            + pltpu.roll(part, LANES - 2 * HEAD, 1)
            + pltpu.roll(part, LANES - 4 * HEAD, 1)
        )
        if previous is not None:
            kept, tail = previous
            tail = tail + pltpu.roll(summed, LANES - HEAD, 1)
            own.append(jnp.where(lane < span - HEAD, kept, tail))
        previous = part, summed
    pairs = []
    for index in range(0, slots + 2, 2):
        pairs.append(jnp.where(lane < span, own[index], pltpu.roll(own[index + 1], span, 1)))
    turned = turn(pairs[:blocks])
    for index, value in enumerate(turned + pairs[blocks:]):
        out_ref[:, LANES * index : LANES * (index + 1)] = flip(value)[:channels].astype(BF)
    fetch.wait()


def arrange(arrived, templates, slots, stride, channels):
    return pl.pallas_call(
        functools.partial(arrange_kernel, slots, stride),
        out_shape=[
            jax.ShapeDtypeStruct((channels, (slots // 2 + 1) * LANES), BF),
            jax.ShapeDtypeStruct((channels // 3, *templates.shape[1:]), BF),
        ],
        in_specs=[whole(), whole(pltpu.HBM)],
        out_specs=[whole(), whole()],
        scratch_shapes=[pltpu.SemaphoreType.DMA],
        compiler_params=pltpu.CompilerParams(vmem_limit_bytes=50 * MIB),
    )(arrived, templates)


def regroup_kernel(template_hbm, out_hbm, held, turned, arrivals, departures):
    kept, channels = template_hbm.shape[:2]
    quarter = channels // lax.axis_size("tmpl")
    parts = range(0, channels, CHUNK)

    def fetch(first):
        part = slice(first, first + CHUNK)
        return pltpu.make_async_copy(template_hbm.at[:, part, :], held.at[:, part, :], arrivals.at[first // CHUNK])

    fetches = [fetch(first) for first in parts]
    for copy in fetches:
        copy.start()
    sends = []
    for first, copy in zip(parts, fetches):
        copy.wait()
        for row in range(0, kept, CHUNK):
            rows = slice(row, row + CHUNK)
            turned[first : first + CHUNK, rows, :] = jnp.swapaxes(held[rows, first : first + CHUNK, :], 0, 1)
        if first == 0:
            me = lax.axis_index("tmpl")
        edge = min((first // quarter + 1) * quarter, first + CHUNK)
        for start, stop in ((first, edge), (edge, first + CHUNK)):
            if start == stop:
                continue
            place = (me ^ (start // quarter)) * quarter + start % quarter
            sends.append(
                pltpu.make_async_copy(
                    turned.at[start:stop], out_hbm.at[pl.ds(place, stop - start)], departures.at[len(sends)]
                )
            )
            sends[-1].start()
    for copy in sends:
        copy.wait()


def regroup(templates):
    kept, channels, tlen = templates.shape
    turned = (channels, kept, tlen)
    return pl.pallas_call(
        regroup_kernel,
        in_specs=[whole(pltpu.HBM)],
        out_specs=whole(pltpu.HBM),
        out_shape=jax.ShapeDtypeStruct(turned, BF),
        scratch_shapes=[
            pltpu.VMEM(templates.shape, BF),
            pltpu.VMEM(turned, BF),
            pltpu.SemaphoreType.DMA((channels // CHUNK,)),
            pltpu.SemaphoreType.DMA((channels // CHUNK + lax.axis_size("tmpl"),)),
        ],
        compiler_params=pltpu.CompilerParams(vmem_limit_bytes=56 * MIB),
        cost_estimate=pl.CostEstimate(flops=2 * templates.size, bytes_accessed=4 * templates.size, transcendentals=0),
    )(templates)


def shifted(here, there, row, out):
    step = lax.broadcasted_iota(jnp.int32, (8, LANES), 0)
    within = lane_of((8, LANES)) % CHUNK
    blocks = out.shape[1] // CHUNK
    for side in range(2):
        for block in range(blocks):
            one = jnp.broadcast_to(here[block, pl.ds(row + side, 1), :], (8, LANES))
            other = jnp.broadcast_to(there[block + 1, pl.ds(row + side, 1), :], (8, LANES))
            halves = [
                pltpu.roll(jnp.where(within < CHUNK - first - step, one, other), first, 1, stride=1, stride_axis=0)
                for first in (0, 8)
            ]
            out[side, CHUNK * block : CHUNK * (block + 1), :] = jnp.concatenate(halves, 0).astype(BF)


def correlate_kernel(steps, begun, *refs):
    refs = list(refs)
    samples = [refs.pop(0) for _ in steps]
    template_hbm = refs.pop(0)
    first_ref = refs.pop(0)
    begun_refs = [refs.pop(0) for _ in range(3 if begun else 0)]
    out_refs = [refs.pop(0) for _ in range(1 if begun else 4)]
    held, *unfolded, even, odd, power, square, total, arrivals, departures = refs
    unfolded = unfolded[:2], unfolded[2:]
    rows = samples[0].shape[0]
    blocks = samples[0].shape[1] // LANES - 1
    channels, kept, tlen = held.shape[1:]
    pairs = channels // 2
    count = len(steps)
    norm = float(CH * tlen)
    lane = lane_of((1, LANES))

    def fetch(start, stop, target, index):
        return pltpu.make_async_copy(template_hbm.at[start:stop], target, arrivals.at[index])

    early = first_ref.shape[0]
    templates = [first_ref] + [held.at[index] for index in range(count - 1)]
    if begun:
        fetches = [
            fetch(step * channels, (step + 1) * channels, held.at[index], index)
            for index, step in enumerate(steps[1:])
        ]
    else:
        fetches = [
            fetch(early, channels, held.at[0, pl.ds(0, channels - early)], 0),
            fetch(channels, 2 * channels, out_refs[3], 1),
        ]
    for copy in fetches if begun else fetches[:1]:
        copy.start()

    def taps_of(index, channel):
        if not begun and channel >= early:
            return held[0, channel - early]
        return templates[index][channel]

    def unfold(index, here, there, block):
        value = samples[index][:, LANES * block : LANES * (block + 1)].astype(F32)
        after = samples[index][:, LANES * blocks :].astype(F32)
        following = jnp.where(
            lane >= LANES - CHUNK,
            pltpu.roll(after, (LANES - CHUNK - CHUNK * block) % LANES, 1),
            pltpu.roll(value, LANES - CHUNK, 1),
        )
        here[block] = value
        here[block + blocks] = following
        there[block] = pltpu.roll(value, LANES - CHUNK, 1)
        there[block + blocks] = pltpu.roll(following, LANES - CHUNK, 1)
        power[block : block + 1] += jnp.sum(value * value, 0, keepdims=True)
        if block == 0:
            power[blocks:] += jnp.sum(after * after, 0, keepdims=True)

    def lag_scale():
        lines = [power[block : block + 1] for block in range(blocks + 1)]
        lines = turn(lines[:blocks]) + lines[blocks:]
        lines = [flip(jnp.broadcast_to(line, (8, LANES)))[0:1] for line in lines]
        later = jnp.concatenate(lines[:blocks], 0)
        earlier = jnp.concatenate(lines[1:], 0)
        step = 1
        while step < LANES:
            later = later + jnp.where(lane < LANES - step, pltpu.roll(later, LANES - step, 1), 0.0)
            earlier = earlier + jnp.where(lane >= step, pltpu.roll(earlier, step, 1), 0.0)
            step *= 2
        earlier = jnp.where(lane >= 1, pltpu.roll(earlier, 1, 1), 0.0)
        return lax.rsqrt((later + earlier) / norm + EPSILON) / norm

    def products(*sums):
        if begun:
            power[...] = begun_refs[1][...]
            square[...] = begun_refs[2][...]
        else:
            power[...] = jnp.zeros_like(power)
            square[...] = jnp.zeros_like(square)
        for block in range(blocks):
            unfold(0, *unfolded[0], block)
        shifted(*unfolded[0], 0, even)
        for index in range(count):
            side = index % 2
            if index > 0:
                fetches[index - 1].wait()
            for pair in range(pairs):
                now, then = (even, odd) if pair % 2 == 0 else (odd, even)
                if not begun and 2 * pair == early:
                    fetches[0].wait()
                    fetches[1].start()
                taps = [taps_of(index, 2 * pair + half) for half in range(2)]
                square[...] += sum(jnp.square(tap.astype(F32)) for tap in taps)
                taps = jnp.concatenate(taps, 1)
                for stage in range(2):
                    for unit in range(2):
                        first = 2 * (2 * unit + stage)
                        columns = [
                            jnp.concatenate(
                                [now[half, CHUNK * block : CHUNK * block + tlen, :] for half in range(2)], 0
                            )
                            for block in (first, first + 1)
                        ]
                        pltpu.matmul_push_rhs(jnp.concatenate(columns, 1), stage, unit)
                    for unit in range(2):
                        pltpu.matmul_acc_lhs(sums[2 * unit + stage], taps, load_staged_rhs=stage)
                if pair < blocks and index < count - 1:
                    unfold(index + 1, *unfolded[1 - side], pair)
                if pair < pairs - 1:
                    shifted(*unfolded[side], 2 * (pair + 1), then)
                elif index < count - 1:
                    shifted(*unfolded[1 - side], 0, then)
        results = []
        for index, ref in enumerate(sums):
            value = pltpu.matmul_pop(ref)
            if begun:
                value = value + begun_refs[0][:, 2 * LANES * index : 2 * LANES * (index + 1)]
            results += [value[:, :LANES], value[:, LANES:]]
        if not begun:
            for block, value in enumerate(results):
                out_refs[0][:, LANES * block : LANES * (block + 1)] = value
            out_refs[1][...] = power[...]
            out_refs[2][...] = square[...]
            fetches[1].wait()
            return
        scale = lag_scale()
        template_scale = lax.rsqrt(jnp.sum(square[...], 1, keepdims=True) / norm + EPSILON)
        height = kept // departures.shape[0]
        copies = []
        for part in range(departures.shape[0]):
            span = slice(part * height, (part + 1) * height)
            for block, value in enumerate(turn([result[span] for result in results])):
                total[span, LANES * block : LANES * (block + 1)] = (
                    flip(value) * template_scale[span] * scale[block : block + 1, :]
                )
            copies.append(pltpu.make_async_copy(total.at[span], out_refs[0].at[span], departures.at[part]))
            copies[-1].start()
        for copy in copies:
            copy.wait()

    pl.run_scoped(
        products, *[pltpu.ACC(unit)((kept, 2 * LANES), F32) for unit in (0, 0, 1, 1)]
    )


def correlate(steps, samples, templates, first, begun=()):
    channels, kept, tlen = templates.shape
    channels //= lax.axis_size("tmpl")
    rows = samples[0].shape[0]
    blocks = samples[0].shape[1] // LANES - 1
    here = pltpu.VMEM((2 * blocks, rows, LANES), F32)
    shifts = pltpu.VMEM((2, CHUNK * (2 * blocks - 1), LANES), BF)
    result = jax.ShapeDtypeStruct((kept, blocks * LANES), F32)
    power = jax.ShapeDtypeStruct((blocks + 1, LANES), F32)
    square = jax.ShapeDtypeStruct((kept, tlen), F32)
    count = len(steps)
    held = (channels, kept, tlen)
    return pl.pallas_call(
        functools.partial(correlate_kernel, steps, bool(begun)),
        out_shape=result if begun else [result, power, square, jax.ShapeDtypeStruct(held, BF)],
        in_specs=[whole()] * count + [whole(pltpu.HBM)] + [whole()] * (1 + len(begun)),
        out_specs=whole(pltpu.HBM) if begun else [whole()] * 4,
        scratch_shapes=[
            pltpu.VMEM((max(count - 1, 1), *held), BF),
            *[here] * 4,
            shifts,
            shifts,
            pltpu.VMEM(power.shape, F32),
            pltpu.VMEM(square.shape, F32),
            pltpu.VMEM(result.shape if begun else (8, LANES), F32),
            pltpu.SemaphoreType.DMA((2,)),
            pltpu.SemaphoreType.DMA((4,)),
        ],
        compiler_params=pltpu.CompilerParams(vmem_limit_bytes=(50 if begun else 46) * MIB),
        cost_estimate=pl.CostEstimate(
            flops=2 * kept * blocks * LANES * count * channels * tlen,
            bytes_accessed=2 * count * channels * kept * tlen,
            transcendentals=0,
        ),
    )(*samples, templates, first, *begun)


def shards(records, band_filter, templates, destinations, offsets, live_counts):
    windows = lax.axis_size("tm")
    quarters = lax.axis_size("tmpl")
    entries, rec_len = records.shape[1:]
    channels = CH // quarters
    slots = entries // channels
    stride = 2 * (entries // windows)
    outgoing = pack(records, band_filter, destinations, offsets, live_counts, slots, windows)
    outgoing = outgoing.reshape(windows, stride, LANES)
    arrived = lax.all_to_all(outgoing, "tm", split_axis=0, concat_axis=0, tiled=True)
    grouped = regroup(templates)
    own, first = arrange(arrived.reshape(2 * entries, LANES), grouped, slots, stride, channels)
    steps = tuple(range(1, quarters))
    samples = [
        lax.ppermute(own, "tmpl", [(source, source ^ step) for source in range(quarters)]) for step in steps
    ]
    *begun, first = correlate((0,), [own], grouped, first)
    return correlate(steps, samples, grouped, first, begun)


def solution(mesh):
    in_specs = (
        P("tmpl", "tm", None),
        P(),
        P("tmpl", None, None),
        P("tmpl", "tm"),
        P("tmpl", "tm"),
        P("tmpl", "tm"),
    )
    out_specs = P("tmpl", "tm")
    inner = jax.shard_map(shards, mesh=mesh, in_specs=in_specs, out_specs=out_specs, check_vma=False)
    return inner
```

```python
import functools

import jax
import jax.numpy as jnp
from jax import lax
from jax.experimental import pallas as pl
from jax.experimental.pallas import tpu as pltpu
from jax.sharding import PartitionSpec as P

CH = 144
DEC = 8
TAPS = 65
EPSILON = 1e-06

LANES = 128
CHUNK = 16
HEAD = (TAPS - 1) // DEC
MIB = 2**20
BF = jnp.bfloat16
F32 = jnp.float32


def whole(space=pltpu.VMEM):
    return pl.BlockSpec(memory_space=space)


def lane_of(shape):
    return lax.broadcasted_iota(jnp.int32, shape, len(shape) - 1)


def flip(values):
    lane = lane_of(values.shape)
    return jnp.take_along_axis(values, lane + (CHUNK - 1) - 2 * (lane % CHUNK), 1)


def turn(rows):
    chunk = lane_of((1, LANES)) // CHUNK
    rows = list(rows)
    step = 1
    while step < len(rows):
        odd = (chunk // step) % 2 == 1
        shift = CHUNK * step
        for low in range(len(rows)):
            if low & step:
                continue
            first, second = rows[low], rows[low + step]
            rows[low] = jnp.where(odd, pltpu.roll(second, shift, 1), first)
            rows[low + step] = jnp.where(odd, second, pltpu.roll(first, LANES - shift, 1))
        step *= 2
    return rows


def pack_kernel(
    slots,
    windows,
    live_hbm,
    record_hbm,
    band_hbm,
    window_hbm,
    start_hbm,
    out_ref,
    live_ref,
    record_ref,
    band_ref,
    window_ref,
    start_ref,
    taps,
    labels,
    before,
    arrivals,
):
    entries, rec_len = record_ref.shape[1:]
    span = rec_len // DEC
    capacity = entries // windows
    stride = 2 * capacity
    width = taps.shape[1]
    copies = [
        pltpu.make_async_copy(source, target, arrivals.at[index])
        for index, (source, target) in enumerate(
            [
                (band_hbm, band_ref),
                (window_hbm, window_ref),
                (start_hbm, start_ref),
                (live_hbm, live_ref),
                (record_hbm, record_ref),
            ]
        )
    ]
    for copy in copies:
        copy.start()

    before[...] = jnp.where(
        lax.broadcasted_iota(jnp.int32, before.shape, 0) <= lane_of(before.shape), 1.0, 0.0
    ).astype(BF)
    taps[...] = jnp.zeros_like(taps)
    labels[...] = jnp.zeros_like(labels)
    for copy in copies[:4]:
        copy.wait()
    taps[0:1, 0:TAPS] = band_ref[...].reshape(1, TAPS)
    base = jnp.broadcast_to(taps[0:1, :], taps.shape)
    firsts = list(range(HEAD, HEAD + span, 8)) + [0, span, 0, span, 0]
    bands = [
        pltpu.roll(base, (DEC * first - DEC * HEAD) % width, 1, stride=DEC, stride_axis=0)[:, :rec_len]
        for first in firsts
    ]
    bands.append(jnp.zeros((LANES - 8 * len(firsts), rec_len), F32))
    filters = jnp.concatenate(bands, 0)
    filter_high = filters.astype(BF)
    filter_low = (filters - filter_high.astype(F32)).astype(BF)
    filters = jnp.concatenate([filter_high, filter_low], 0)

    window = window_ref[...]
    label = start_ref[...] // rec_len
    channel = label // slots
    slot = label - channel * slots
    mark = span + 5 * HEAD
    labels[mark : mark + 1, 0:entries] = (slot + 1).astype(F32)
    labels[mark + 1 : mark + 2, 0:entries] = channel.astype(F32)
    marks = labels[...].T[:entries]
    live = lane_of((1, entries)) < live_ref[0, 0]
    each = lax.broadcasted_iota(jnp.int32, (windows, entries), 0)
    member = (window == each) & live
    ahead = (window == each + 1) & live & (slot < 3)
    both = jnp.concatenate([jnp.where(member, 1.0, 0.0), jnp.where(ahead, 1.0, 0.0)], 0)
    count = jnp.dot(both.astype(BF), before[...], preferred_element_type=F32)
    first = (each * stride).astype(F32)
    place = jnp.sum(jnp.where(member, count[:windows] + first, 0.0), 0, keepdims=True) - 1.0
    place_ahead = (
        jnp.sum(jnp.where(ahead, count[windows:] + (first + capacity), 0.0), 0, keepdims=True) - 1.0
    )

    copies[4].wait()
    contract = (((1,), (1,)), ((), ()))
    record = record_ref[0]
    record_high = record.astype(BF)
    record_low = (record - record_high.astype(F32)).astype(BF)
    upper = lax.dot_general(record_high, filters, contract, preferred_element_type=F32)
    lower = lax.dot_general(record_low, filters, contract, preferred_element_type=F32)
    value = upper[:, :LANES] + (upper[:, LANES:] + (lower[:, :LANES] + lower[:, LANES:]))
    high = value.astype(BF).astype(F32)
    rest = value - high
    middle = rest.astype(BF).astype(F32)
    low = rest - middle
    lane = lane_of(value.shape)
    payload = jnp.where(
        lane < span + HEAD,
        high,
        jnp.where(lane < span + 3 * HEAD, middle, jnp.where(lane < mark, low, marks)),
    ).astype(BF)

    total = out_ref.shape[0]
    plain = capacity % 8 == 0
    part = stride if plain else total // 4
    row = lax.broadcasted_iota(jnp.int32, (part, entries), 0).astype(F32)
    for index in range(total // part):
        here, there = place - float(index * part), place_ahead - float(index * part)
        if plain:
            chosen = jnp.concatenate(
                [
                    jnp.where(row[:capacity] == here, 1.0, 0.0),
                    jnp.where(row[capacity:] == there, 1.0, 0.0),
                ],
                0,
            )
        else:
            chosen = jnp.where((row == here) | (row == there), 1.0, 0.0)
        out_ref[index * part : (index + 1) * part, :] = jnp.dot(
            chosen.astype(BF), payload, preferred_element_type=F32
        ).astype(BF)


def pack(records, band_filter, windows_of, starts, live, slots, windows):
    entries, rec_len = records.shape[1:]
    return pl.pallas_call(
        functools.partial(pack_kernel, slots, windows),
        out_shape=jax.ShapeDtypeStruct((2 * entries, LANES), BF),
        in_specs=[whole(pltpu.HBM)] * 5,
        out_specs=whole(),
        scratch_shapes=[
            pltpu.SMEM(live.shape, live.dtype),
            pltpu.VMEM(records.shape, F32),
            pltpu.VMEM(band_filter.shape, F32),
            pltpu.VMEM(windows_of.shape, windows_of.dtype),
            pltpu.VMEM(starts.shape, starts.dtype),
            pltpu.VMEM((8, rec_len + LANES), F32),
            pltpu.VMEM((LANES, pl.cdiv(entries, LANES) * LANES), F32),
            pltpu.VMEM((entries, entries), BF),
            pltpu.SemaphoreType.DMA((5,)),
        ],
        compiler_params=pltpu.CompilerParams(vmem_limit_bytes=60 * MIB),
    )(live, records, band_filter, windows_of, starts)


def arrange_kernel(slots, stride, arrived_ref, template_hbm, out_ref, held_ref, arrival):
    fetch = pltpu.make_async_copy(template_hbm.at[: held_ref.shape[0]], held_ref, arrival)
    fetch.start()
    total = arrived_ref.shape[0]
    channels = out_ref.shape[0]
    rows = pl.cdiv(channels, 8) * 8
    blocks = out_ref.shape[1] // LANES - 1
    span = LANES // 2
    mark = span + 5 * HEAD
    arrived = arrived_ref[...].astype(F32)
    capacity = stride // 2
    lane = lane_of((8, LANES))
    weigh = jnp.where(lane == mark, float(rows), jnp.where(lane == mark + 1, 1.0, 0.0)).astype(BF)
    placed = []
    for side, count in enumerate((slots, 3)):
        values = jnp.concatenate(
            [
                arrived[first : first + capacity]
                for first in range(side * capacity, total, stride)
            ],
            0,
        ).astype(BF)
        name = lax.dot_general(weigh, values, (((1,), (1,)), ((), ())), preferred_element_type=F32)[0:1]
        row = lax.broadcasted_iota(jnp.int32, (count * rows, total // 2), 0).astype(F32)
        chosen = jnp.where(row == name - float(rows), 1.0, 0.0).astype(BF)
        placed.append(jnp.dot(chosen, values, preferred_element_type=F32))
    placed = jnp.concatenate(placed, 0)
    held = slots + 3
    lane = lane_of((rows, LANES))
    own = []
    previous = None
    for slot in range(held):
        part = placed[slot * rows : (slot + 1) * rows]
        summed = (
            part
            + pltpu.roll(part, LANES - 2 * HEAD, 1)
            + pltpu.roll(part, LANES - 4 * HEAD, 1)
        )
        if previous is not None:
            kept, tail = previous
            tail = tail + pltpu.roll(summed, LANES - HEAD, 1)
            own.append(jnp.where(lane < span - HEAD, kept, tail))
        previous = part, summed
    pairs = []
    for index in range(0, slots + 2, 2):
        pairs.append(jnp.where(lane < span, own[index], pltpu.roll(own[index + 1], span, 1)))
    turned = turn(pairs[:blocks])
    for index, value in enumerate(turned + pairs[blocks:]):
        out_ref[:, LANES * index : LANES * (index + 1)] = flip(value)[:channels].astype(BF)
    fetch.wait()


def arrange(arrived, templates, slots, stride, channels):
    return pl.pallas_call(
        functools.partial(arrange_kernel, slots, stride),
        out_shape=[
            jax.ShapeDtypeStruct((channels, (slots // 2 + 1) * LANES), BF),
            jax.ShapeDtypeStruct((channels // 6, *templates.shape[1:]), BF),
        ],
        in_specs=[whole(), whole(pltpu.HBM)],
        out_specs=[whole(), whole()],
        scratch_shapes=[pltpu.SemaphoreType.DMA],
        compiler_params=pltpu.CompilerParams(vmem_limit_bytes=50 * MIB),
    )(arrived, templates)


def regroup_kernel(template_hbm, out_hbm, held, turned, arrivals, departures):
    kept, channels = template_hbm.shape[:2]
    quarter = channels // lax.axis_size("tmpl")
    parts = range(0, channels, CHUNK)

    def fetch(first):
        part = slice(first, first + CHUNK)
        return pltpu.make_async_copy(template_hbm.at[:, part, :], held.at[:, part, :], arrivals.at[first // CHUNK])

    fetches = [fetch(first) for first in parts]
    for copy in fetches:
        copy.start()
    sends = []
    for first, copy in zip(parts, fetches):
        copy.wait()
        for row in range(0, kept, CHUNK):
            rows = slice(row, row + CHUNK)
            turned[first : first + CHUNK, rows, :] = jnp.swapaxes(held[rows, first : first + CHUNK, :], 0, 1)
        if first == 0:
            me = lax.axis_index("tmpl")
        edge = min((first // quarter + 1) * quarter, first + CHUNK)
        for start, stop in ((first, edge), (edge, first + CHUNK)):
            if start == stop:
                continue
            place = (me ^ (start // quarter)) * quarter + start % quarter
            sends.append(
                pltpu.make_async_copy(
                    turned.at[start:stop], out_hbm.at[pl.ds(place, stop - start)], departures.at[len(sends)]
                )
            )
            sends[-1].start()
    for copy in sends:
        copy.wait()


def regroup(templates):
    kept, channels, tlen = templates.shape
    turned = (channels, kept, tlen)
    return pl.pallas_call(
        regroup_kernel,
        in_specs=[whole(pltpu.HBM)],
        out_specs=whole(pltpu.HBM),
        out_shape=jax.ShapeDtypeStruct(turned, BF),
        scratch_shapes=[
            pltpu.VMEM(templates.shape, BF),
            pltpu.VMEM(turned, BF),
            pltpu.SemaphoreType.DMA((channels // CHUNK,)),
            pltpu.SemaphoreType.DMA((channels // CHUNK + lax.axis_size("tmpl"),)),
        ],
        compiler_params=pltpu.CompilerParams(vmem_limit_bytes=56 * MIB),
        cost_estimate=pl.CostEstimate(flops=2 * templates.size, bytes_accessed=4 * templates.size, transcendentals=0),
    )(templates)


def shifted(here, there, row, out):
    step = lax.broadcasted_iota(jnp.int32, (8, LANES), 0)
    within = lane_of((8, LANES)) % CHUNK
    blocks = out.shape[1] // CHUNK
    for side in range(2):
        for block in range(blocks):
            one = jnp.broadcast_to(here[block, pl.ds(row + side, 1), :], (8, LANES))
            other = jnp.broadcast_to(there[block + 1, pl.ds(row + side, 1), :], (8, LANES))
            halves = [
                pltpu.roll(jnp.where(within < CHUNK - first - step, one, other), first, 1, stride=1, stride_axis=0)
                for first in (0, 8)
            ]
            out[side, CHUNK * block : CHUNK * (block + 1), :] = jnp.concatenate(halves, 0).astype(BF)


def correlate_kernel(steps, begun, *refs):
    refs = list(refs)
    samples = [refs.pop(0) for _ in steps]
    template_hbm = refs.pop(0)
    first_ref = refs.pop(0)
    begun_refs = [refs.pop(0) for _ in range(3 if begun else 0)]
    out_refs = [refs.pop(0) for _ in range(1 if begun else 4)]
    held, *unfolded, even, odd, power, square, total, arrivals, departures = refs
    unfolded = unfolded[:2], unfolded[2:]
    rows = samples[0].shape[0]
    blocks = samples[0].shape[1] // LANES - 1
    channels, kept, tlen = held.shape[1:]
    pairs = channels // 2
    count = len(steps)
    norm = float(CH * tlen)
    lane = lane_of((1, LANES))

    def fetch(start, stop, target, index):
        return pltpu.make_async_copy(template_hbm.at[start:stop], target, arrivals.at[index])

    early = first_ref.shape[0]
    templates = [first_ref] + [held.at[index] for index in range(count - 1)]
    if begun:
        fetches = [
            fetch(step * channels, (step + 1) * channels, held.at[index], index)
            for index, step in enumerate(steps[1:])
        ]
    else:
        fetches = [
            fetch(early, channels, held.at[0, pl.ds(0, channels - early)], 0),
            fetch(channels, 2 * channels, out_refs[3], 1),
        ]
    for copy in fetches if begun else fetches[:1]:
        copy.start()

    def taps_of(index, channel):
        if not begun and channel >= early:
            return held[0, channel - early]
        return templates[index][channel]

    def unfold(index, here, there, block):
        value = samples[index][:, LANES * block : LANES * (block + 1)].astype(F32)
        after = samples[index][:, LANES * blocks :].astype(F32)
        following = jnp.where(
            lane >= LANES - CHUNK,
            pltpu.roll(after, (LANES - CHUNK - CHUNK * block) % LANES, 1),
            pltpu.roll(value, LANES - CHUNK, 1),
        )
        here[block] = value
        here[block + blocks] = following
        there[block] = pltpu.roll(value, LANES - CHUNK, 1)
        there[block + blocks] = pltpu.roll(following, LANES - CHUNK, 1)
        power[block : block + 1] += jnp.sum(value * value, 0, keepdims=True)
        if block == 0:
            power[blocks:] += jnp.sum(after * after, 0, keepdims=True)

    def lag_scale():
        lines = [power[block : block + 1] for block in range(blocks + 1)]
        lines = turn(lines[:blocks]) + lines[blocks:]
        lines = [flip(jnp.broadcast_to(line, (8, LANES)))[0:1] for line in lines]
        later = jnp.concatenate(lines[:blocks], 0)
        earlier = jnp.concatenate(lines[1:], 0)
        step = 1
        while step < LANES:
            later = later + jnp.where(lane < LANES - step, pltpu.roll(later, LANES - step, 1), 0.0)
            earlier = earlier + jnp.where(lane >= step, pltpu.roll(earlier, step, 1), 0.0)
            step *= 2
        earlier = jnp.where(lane >= 1, pltpu.roll(earlier, 1, 1), 0.0)
        return lax.rsqrt((later + earlier) / norm + EPSILON) / norm

    def products(*sums):
        if begun:
            power[...] = begun_refs[1][...]
            square[...] = begun_refs[2][...]
        else:
            power[...] = jnp.zeros_like(power)
            square[...] = jnp.zeros_like(square)
        for block in range(blocks):
            unfold(0, *unfolded[0], block)
        shifted(*unfolded[0], 0, even)
        for index in range(count):
            side = index % 2
            if index > 0:
                fetches[index - 1].wait()
            for pair in range(pairs):
                now, then = (even, odd) if pair % 2 == 0 else (odd, even)
                if not begun and 2 * pair == early:
                    fetches[0].wait()
                    fetches[1].start()
                taps = [taps_of(index, 2 * pair + half) for half in range(2)]
                square[...] += sum(jnp.square(tap.astype(F32)) for tap in taps)
                taps = jnp.concatenate(taps, 1)
                for stage in range(2):
                    for unit in range(2):
                        first = 2 * (2 * unit + stage)
                        columns = [
                            jnp.concatenate(
                                [now[half, CHUNK * block : CHUNK * block + tlen, :] for half in range(2)], 0
                            )
                            for block in (first, first + 1)
                        ]
                        pltpu.matmul_push_rhs(jnp.concatenate(columns, 1), stage, unit)
                    for unit in range(2):
                        pltpu.matmul_acc_lhs(sums[2 * unit + stage], taps, load_staged_rhs=stage)
                if pair < blocks and index < count - 1:
                    unfold(index + 1, *unfolded[1 - side], pair)
                if pair < pairs - 1:
                    shifted(*unfolded[side], 2 * (pair + 1), then)
                elif index < count - 1:
                    shifted(*unfolded[1 - side], 0, then)
        results = []
        for index, ref in enumerate(sums):
            value = pltpu.matmul_pop(ref)
            if begun:
                value = value + begun_refs[0][:, 2 * LANES * index : 2 * LANES * (index + 1)]
            results += [value[:, :LANES], value[:, LANES:]]
        if not begun:
            for block, value in enumerate(results):
                out_refs[0][:, LANES * block : LANES * (block + 1)] = value
            out_refs[1][...] = power[...]
            out_refs[2][...] = square[...]
            fetches[1].wait()
            return
        scale = lag_scale()
        template_scale = lax.rsqrt(jnp.sum(square[...], 1, keepdims=True) / norm + EPSILON)
        height = kept // departures.shape[0]
        copies = []
        for part in range(departures.shape[0]):
            span = slice(part * height, (part + 1) * height)
            for block, value in enumerate(turn([result[span] for result in results])):
                total[span, LANES * block : LANES * (block + 1)] = (
                    flip(value) * template_scale[span] * scale[block : block + 1, :]
                )
            copies.append(pltpu.make_async_copy(total.at[span], out_refs[0].at[span], departures.at[part]))
            copies[-1].start()
        for copy in copies:
            copy.wait()

    pl.run_scoped(
        products, *[pltpu.ACC(unit)((kept, 2 * LANES), F32) for unit in (0, 0, 1, 1)]
    )


def correlate(steps, samples, templates, first, begun=()):
    channels, kept, tlen = templates.shape
    channels //= lax.axis_size("tmpl")
    rows = samples[0].shape[0]
    blocks = samples[0].shape[1] // LANES - 1
    here = pltpu.VMEM((2 * blocks, rows, LANES), F32)
    shifts = pltpu.VMEM((2, CHUNK * (2 * blocks - 1), LANES), BF)
    result = jax.ShapeDtypeStruct((kept, blocks * LANES), F32)
    power = jax.ShapeDtypeStruct((blocks + 1, LANES), F32)
    square = jax.ShapeDtypeStruct((kept, tlen), F32)
    count = len(steps)
    held = (channels, kept, tlen)
    return pl.pallas_call(
        functools.partial(correlate_kernel, steps, bool(begun)),
        out_shape=result if begun else [result, power, square, jax.ShapeDtypeStruct(held, BF)],
        in_specs=[whole()] * count + [whole(pltpu.HBM)] + [whole()] * (1 + len(begun)),
        out_specs=whole(pltpu.HBM) if begun else [whole()] * 4,
        scratch_shapes=[
            pltpu.VMEM((max(count - 1, 1), *held), BF),
            *[here] * 4,
            shifts,
            shifts,
            pltpu.VMEM(power.shape, F32),
            pltpu.VMEM(square.shape, F32),
            pltpu.VMEM(result.shape if begun else (8, LANES), F32),
            pltpu.SemaphoreType.DMA((2,)),
            pltpu.SemaphoreType.DMA((4,)),
        ],
        compiler_params=pltpu.CompilerParams(vmem_limit_bytes=(50 if begun else 46) * MIB),
        cost_estimate=pl.CostEstimate(
            flops=2 * kept * blocks * LANES * count * channels * tlen,
            bytes_accessed=2 * count * channels * kept * tlen,
            transcendentals=0,
        ),
    )(*samples, templates, first, *begun)


def shards(records, band_filter, templates, destinations, offsets, live_counts):
    windows = lax.axis_size("tm")
    quarters = lax.axis_size("tmpl")
    entries, rec_len = records.shape[1:]
    channels = CH // quarters
    slots = entries // channels
    stride = 2 * (entries // windows)
    outgoing = pack(records, band_filter, destinations, offsets, live_counts, slots, windows)
    outgoing = outgoing.reshape(windows, stride, LANES)
    arrived = lax.all_to_all(outgoing, "tm", split_axis=0, concat_axis=0, tiled=True)
    grouped = regroup(templates)
    own, first = arrange(arrived.reshape(2 * entries, LANES), grouped, slots, stride, channels)
    steps = tuple(range(1, quarters))
    samples = [
        lax.ppermute(own, "tmpl", [(source, source ^ step) for source in range(quarters)]) for step in steps
    ]
    *begun, first = correlate((0,), [own], grouped, first)
    return correlate(steps, samples, grouped, first, begun)


def solution(mesh):
    in_specs = (
        P("tmpl", "tm", None),
        P(),
        P("tmpl", None, None),
        P("tmpl", "tm"),
        P("tmpl", "tm"),
        P("tmpl", "tm"),
    )
    out_specs = P("tmpl", "tm")
    inner = jax.shard_map(shards, mesh=mesh, in_specs=in_specs, out_specs=out_specs, check_vma=False)
    return inner
```
